256 devices in a mesh: band: 8 (over z), pw: 32 (over x, y, core).
Axes of the slice: x: 4, y: 4, z: 8, core: 2. Of those that a mesh axis runs over, the one named last changes fastest.
Arguments:
- coeffs: float32 [2, 16, 114688], P(None, 'band', 'pw'), may hold values from -6 to 6
- occupation: float32 [16], P('band'), may hold values from 0.5 to 2
- stick_columns: int32 [3072], replicated, may hold values from 0 to 16383, as said below
- sphere_slots: int32 [114688], P('pw'), may hold values from 0 to 12287, as said below
- atom_sites: int32 [3, 1000], replicated, may hold values from 0 to 127
Outputs:
- new_coeffs: float32 [2, 16, 114688], P(None, 'band', 'pw')
- density: float32 [128, 128, 128], P('pw')
The draws below stay inside these ranges and needn't reach their ends.
Inputs may be any that keep to these rules, and one draw needn't show every extreme that they name: `stick_columns`: all entries are distinct; each column's wrapped frequencies satisfy w(x)^2 + w(y)^2 <= 32^2. `sphere_slots`: within one block of 3584 entries the values are distinct; each names a point with w(x)^2 + w(y)^2 + w(z)^2 <= 32^2.
All inputs are finite; a program needn't handle non-finite values.
Results may differ from the reference program's by a relative error of at most 0.0003.
Values sent between devices are 32-bit elements; how exact they have to be, the bound alone decides.
A program may use at most 64 MiB of HBM per device.

```python
import math
import jax
import jax.numpy as jnp
import numpy as np
from jax import lax

NG = 128
NST_DEV = 96
NPW_DEV = 3584
NORB_DEV = 2
NATOM = 1000
NST = 3072
NPW = 114688
NORB = 16
N_BAND = 8
N_PW = 32


def permute_row(row_key, values):
    return values[jax.random.permutation(row_key, values.shape[0])]


def stick_layout(key):
    devices = NST // NST_DEV
    radius = NG // 4
    counter = np.arange(NG)
    wrap = np.where(counter < NG // 2, counter, counter - NG)
    rho = (wrap[:, None] ** 2 + wrap[None, :] ** 2).reshape(-1)
    inside = np.arange(NG * NG)[rho <= radius * radius]
    lengths = 2 * np.floor(np.sqrt(radius * radius - rho[inside])) + 1
    ordered = inside[np.argsort(-lengths, kind='stable')][:NST]
    tiers = jnp.asarray(ordered.reshape(NST_DEV, devices), jnp.int32)
    tier_keys = jax.random.split(jax.random.fold_in(key, 7), NST_DEV)
    dealt = jax.vmap(permute_row)(tier_keys, tiers)
    per_device = jnp.transpose(dealt)
    device_keys = jax.random.split(jax.random.fold_in(key, 9), devices)
    return jax.vmap(permute_row)(device_keys, per_device).astype(jnp.int32)


def draw_stick_columns(key, part):
    return stick_layout(key).reshape(-1)


def draw_sphere_slots(key, part):
    layout = stick_layout(key)
    devices = layout.shape[0]
    radius = NG // 4
    cells = NST_DEV * NG
    counter = jnp.arange(NG, dtype=jnp.int32)
    zwrap = jnp.where(counter < NG // 2, counter, counter - NG)
    xcoord = layout // NG
    ycoord = layout % NG
    xwrap = jnp.where(xcoord < NG // 2, xcoord, xcoord - NG)
    ywrap = jnp.where(ycoord < NG // 2, ycoord, ycoord - NG)
    reach = (xwrap * xwrap + ywrap * ywrap)[:, :, None] + (zwrap * zwrap)[None, None, :]
    outside = (reach > radius * radius).astype(jnp.int32).reshape(devices, cells)
    noise = jax.random.randint(jax.random.fold_in(key, 11), (devices, cells), 0, 2 ** 15)
    slot_index = jnp.arange(cells, dtype=jnp.int32)
    edge = ((slot_index == 0) | (slot_index == cells - 1))[None, :]
    level = jnp.where(edge, -1, outside * 2 ** 15 + noise)
    score = level * cells + slot_index[None, :]
    chosen = jnp.argsort(score, axis=1)[:, :NPW_DEV]
    return chosen.astype(jnp.int32).reshape(-1)


def plant(drawn, rng, least, high):
    longest = drawn.shape.index(max(drawn.shape))
    spots = []
    for shift in (0, 1):
        where = [jax.random.randint(jax.random.fold_in(rng, axis), (), 0, length) for axis, length in enumerate(drawn.shape)]
        where[longest] = (where[longest] + shift) % drawn.shape[longest]
        spots.append(tuple(where))
    return drawn.at[spots[0]].set(least).at[spots[1]].set(high)


def levels(rng, shape, shards, least, largest):
    factor_of, own = 1.0, jax.random.fold_in(rng, 6)
    for axis_at, shards_of in shards:
        draws = jnp.exp(jax.random.uniform(jax.random.fold_in(own, axis_at), (shards_of,), jnp.float32, least / len(shards), largest / len(shards)))
        factor_of = factor_of * jnp.repeat(draws, shape[axis_at] // shards_of).reshape([-1 if axis == axis_at else 1 for axis in range(len(shape))])
    return factor_of


def normal_values(stream_key, shape, scale, most, cuts=(), kind=jnp.bfloat16):
    result = jax.random.normal(stream_key, shape, jnp.float32) * scale
    if len(cuts) > 0:
        result = levels(stream_key, shape, cuts, -0.22, 0.18) * result
    return jnp.clip(result, min=-most, max=most).astype(kind)


def setup_inputs(seed: int = 0) -> dict:
    streams_of = jax.random.split(jax.random.key(seed), 6)
    return {
        "coeffs": normal_values(streams_of[0], (2, NORB, NPW), 1.0, 6.0, ((1, 8), (2, 32)), jnp.float32),
        "occupation": jnp.clip(0.5 + 1.5 * jax.random.uniform(streams_of[1], (NORB,), jnp.float32) ** levels(streams_of[1], (NORB,), ((0, 8),), -0.2, 0.2), 0.5, 2.0),
        "stick_columns": draw_stick_columns(jax.random.fold_in(streams_of[5], 71), 0),
        "sphere_slots": draw_sphere_slots(jax.random.fold_in(streams_of[5], 71), 0),
        "atom_sites": plant(jax.random.randint(streams_of[4], (3, NATOM), 0, NG), jax.random.fold_in(streams_of[4], 1), 0, NG - 1).astype(jnp.int32),
    }


TIME_STEP = 0.2
EPSILON = 1e-06

def wrapped(index):
    return jnp.where(index < NG // 2, index, index - NG)

def kinetic_factor():
    return 123.4 / (NG * NG)

def hartree_factor():
    return 0.1 * NG * NG

def form_factor(ksquare):
    spread_width = NG / 20.0
    return -2.0 * jnp.exp(-ksquare / (2.0 * spread_width * spread_width)) / ((2.0 * math.pi) ** 1.5 * spread_width ** 3)

def phase_table(kvalues, positions):
    angle = 2.0 * math.pi / NG * (kvalues[:, None] * positions[None, :] % NG).astype(jnp.float32)
    return (jnp.cos(angle), -jnp.sin(angle))

def exponential_weights(first_energy, second_energy, spread):
    middle = 0.5 * (first_energy + second_energy)
    half_gap = 0.5 * (first_energy - second_energy)
    radius = jnp.sqrt(half_gap * half_gap + spread * spread)
    cosine = jnp.cos(TIME_STEP * radius)
    sine = jnp.sin(TIME_STEP * radius)
    along_first = sine * half_gap / radius
    along_second = sine * spread / radius
    phase_cos = jnp.cos(TIME_STEP * middle)
    phase_sin = jnp.sin(TIME_STEP * middle)
    weight_first = (phase_cos * cosine - phase_sin * along_first, -phase_cos * along_first - phase_sin * cosine)
    weight_second = (-phase_sin * along_second, -phase_cos * along_second)
    return (weight_first, weight_second)

def reference(coeffs, occupation, stick_columns, sphere_slots, atom_sites):
    total_pw = NPW_DEV * N_PW
    owner = jnp.arange(total_pw, dtype=jnp.int32) // NPW_DEV
    column = stick_columns[owner * NST_DEV + sphere_slots // NG]
    zvalue = sphere_slots % NG
    flat_index = (column * NG + zvalue).astype(jnp.int32)
    kinetic = kinetic_factor() * (wrapped(column // NG) ** 2 + wrapped(column % NG) ** 2 + wrapped(zvalue) ** 2).astype(jnp.float32)
    to_grid = NG ** 3 / math.sqrt(total_pw)
    to_sphere = math.sqrt(total_pw) / NG ** 3

    def to_real(real_part, imag_part):
        grid_re = jnp.zeros((NG ** 3,), jnp.float32).at[flat_index].set(real_part).reshape(NG, NG, NG)
        grid_im = jnp.zeros((NG ** 3,), jnp.float32).at[flat_index].set(imag_part).reshape(NG, NG, NG)
        return jnp.fft.ifftn(lax.complex(grid_re, grid_im)) * to_grid

    def to_sphere_coeffs(field):
        values = jnp.fft.fftn(field).reshape(-1)[flat_index] * to_sphere
        return (jnp.real(values), jnp.imag(values))

    def add_density(total, item):
        real_part, imag_part, weight = item
        field = to_real(real_part, imag_part)
        return (total + weight * (jnp.real(field) ** 2 + jnp.imag(field) ** 2), None)
    density = lax.scan(add_density, jnp.zeros((NG, NG, NG), jnp.float32), (coeffs[0], coeffs[1], occupation))[0]
    density = density / (NORB_DEV * N_BAND)
    counter = jnp.arange(NG, dtype=jnp.int32)
    kwrap = wrapped(counter)
    ksq_int = kwrap[:, None, None] ** 2 + kwrap[None, :, None] ** 2 + kwrap[None, None, :] ** 2
    ksq_float = ksq_int.astype(jnp.float32)
    hartree = jnp.where(ksq_int > 0, hartree_factor() / jnp.maximum(ksq_float, 1.0), 0.0)
    phase_first = phase_table(counter, atom_sites[0])
    phase_second = phase_table(counter, atom_sites[1])
    phase_third = phase_table(counter, atom_sites[2])
    first_c = lax.complex(phase_first[0], phase_first[1])
    second_c = lax.complex(phase_second[0], phase_second[1])
    third_c = lax.complex(phase_third[0], phase_third[1])
    cross = first_c[:, None, :] * third_c[None, :, :]
    structure = jnp.einsum('xza,ya->xyz', cross, second_c, precision=lax.Precision.HIGHEST)
    spectrum = jnp.fft.fftn(density) / NG ** 3
    total_k = hartree * spectrum + form_factor(ksq_float) * structure
    potential = jnp.real(jnp.fft.ifftn(total_k)) * NG ** 3

    def apply(real_part, imag_part, field):
        pot_re, pot_im = to_sphere_coeffs(field * potential)
        return (kinetic * real_part + pot_re, kinetic * imag_part + pot_im)

    def propagate(item):
        coef_re, coef_im = item
        hit_re, hit_im = apply(coef_re, coef_im, to_real(coef_re, coef_im))
        norm_sq = jnp.sum(coef_re * coef_re + coef_im * coef_im) + EPSILON
        norm = jnp.sqrt(norm_sq)
        first_energy = jnp.sum(coef_re * hit_re + coef_im * hit_im) / norm_sq
        rest_re = (hit_re - first_energy * coef_re) / norm
        rest_im = (hit_im - first_energy * coef_im) / norm
        spread = jnp.sqrt(jnp.sum(rest_re * rest_re + rest_im * rest_im) + EPSILON)
        next_re = rest_re / spread
        next_im = rest_im / spread
        again_re, again_im = apply(next_re, next_im, to_real(next_re, next_im))
        second_energy = jnp.sum(next_re * again_re + next_im * again_im)
        weight_first, weight_second = exponential_weights(first_energy, second_energy, spread)
        new_re = weight_first[0] * coef_re - weight_first[1] * coef_im + norm * (weight_second[0] * next_re - weight_second[1] * next_im)
        new_im = weight_first[0] * coef_im + weight_first[1] * coef_re + norm * (weight_second[0] * next_im + weight_second[1] * next_re)
        return (new_re, new_im)
    new_re, new_im = lax.map(propagate, (coeffs[0], coeffs[1]))
    return (jnp.stack([new_re, new_im]), jnp.transpose(density, (2, 0, 1)))
```

```python
import functools
import math

import jax
import jax.numpy as jnp
import numpy as np
import ml_dtypes
from jax import lax
from jax.experimental import pallas as pl
from jax.experimental.pallas import tpu as pltpu
from jax.sharding import PartitionSpec as P

MESH = pl.DeviceIdType.MESH
F32 = jnp.float32
BF16 = jnp.bfloat16

NG = 128
NP = 32
NB = 8
NPW_DEV = 3584
NPW = NPW_DEV * NP
ST = 96
KZ = 80
NR = 24
TIME_STEP = 0.2
EPSILON = 1e-06
STEP = 2.0 * math.pi / NG
WIDTH = NG / 20.0
FORM = -2.0 / ((2.0 * math.pi) ** 1.5 * WIDTH**3)
TO_GRID = 1.0 / math.sqrt(NPW)
TO_SPHERE = math.sqrt(NPW) / NG**3
HARTREE = 0.1 * NG * NG

A1, RS, A2, A3, AGV, AGD, A4, A5, AR = 0, 2, 3, 4, 5, 6, 7, 9, 11
N_SEM = 12


def parts(x):
    hi = x.astype(np.float32).astype(ml_dtypes.bfloat16)
    lo = (x - hi.astype(np.float64)).astype(np.float32).astype(ml_dtypes.bfloat16)
    return hi, lo


def left_table(x):
    hi, lo = parts(x)
    return np.concatenate([hi, hi, lo], axis=1)


def right_table(x):
    hi, lo = parts(x)
    return np.concatenate([hi, hi, lo], axis=0)


def phases(rows, cols):
    angle = STEP * np.mod(np.outer(rows, cols), NG)
    return np.cos(angle), np.sin(angle)


def build_tables():
    grid = np.arange(NG)
    kz_mask = (np.arange(KZ) <= 64).astype(np.float64)
    kz = np.arange(KZ) - 32
    tables = {}
    c, s = phases(grid, kz)
    c, s = c * kz_mask, s * kz_mask
    up = np.zeros((NG, 2, 2, KZ))
    up[:, 0, 0], up[:, 0, 1], up[:, 1, 0], up[:, 1, 1] = c, -s, s, c
    tables["z_up"] = left_table(up.reshape(2 * NG, 2 * KZ))
    down = np.zeros((2, KZ, NG, 2))
    down[0, :, :, 0], down[0, :, :, 1] = c.T, s.T
    down[1, :, :, 0], down[1, :, :, 1] = -s.T, c.T
    tables["z_down"] = left_table(down.reshape(2 * KZ, 2 * NG))

    wy = np.tile(np.arange(64) - 32, (4, 1))
    wy[1, 0] = 32
    y_up = np.zeros((4, 64, 2, 4, NG))
    y_down = np.zeros((4, NG, 2, 4, 64))
    for j in range(4):
        c, s = phases(wy[j], grid)
        y_up[j, :, 0, j], y_up[j, :, 1, j] = c, s
        y_down[j, :, 0, j], y_down[j, :, 1, j] = c.T, s.T
    tables["y_up"] = right_table(y_up.reshape(256, 1024))
    tables["y_down"] = right_table(y_down.reshape(512, 512))

    wx = np.zeros((4, NR))
    xm = np.zeros((4, NR))
    for j in range(4):
        for r in range(16):
            wx[j, r], xm[j, r] = 4 * r + j - 32, 1.0
    wx[0, 16], xm[0, 16] = 32, 1.0
    wx[1, 16], xm[1, 16] = 0, 1.0
    c, s = phases(grid, wx.reshape(-1))
    c, s = c * xm.reshape(-1), s * xm.reshape(-1)
    x_up = np.zeros((2, NG, 2, 4 * NR))
    x_up[0, :, 0], x_up[0, :, 1], x_up[1, :, 0], x_up[1, :, 1] = c, -s, s, c
    tables["x_up"] = left_table(TO_GRID * x_up.reshape(2 * NG, 8 * NR))
    x_down = np.zeros((2, 4 * NR, 2, NG))
    x_down[0, :, 0], x_down[0, :, 1], x_down[1, :, 0], x_down[1, :, 1] = c.T, s.T, -s.T, c.T
    tables["x_down"] = left_table(TO_SPHERE * x_down.reshape(8 * NR, 2 * NG))

    c, s = phases(grid, np.arange(64))
    fwd = np.zeros((NG, 2, 64))
    fwd[:, 0], fwd[:, 1] = c, -s
    sign = np.where(grid % 2 == 0, 1.0, -1.0)
    fwd[:, 1, 0] = sign
    tables["py"] = right_table(fwd.reshape(NG, NG))
    inv = np.zeros((2, 64, NG))
    inv[0], inv[1] = 2.0 * c.T, -2.0 * s.T
    inv[0, 0], inv[1, 0] = 1.0, sign
    tables["piy"] = right_table(inv.reshape(NG, NG))
    c, s = phases(grid, grid)
    tables["px"] = left_table(np.concatenate([c, s], axis=1))
    tables["pix"] = left_table(np.concatenate([c, -s], axis=1))
    pairs = np.concatenate([grid[0::2], grid[1::2]])
    tables["pixp"] = left_table(np.concatenate([c[:, pairs], -s[:, pairs]], axis=1))
    pair = np.eye(2)
    cc, ss = np.kron(c, pair), np.kron(s, pair)
    tables["pz"] = left_table(np.concatenate([cc, ss], axis=1))
    tables["piz"] = left_table(np.concatenate([cc, -ss], axis=1))

    wk = np.where(grid < 64, grid, grid - NG)
    gauss = np.exp(-(wk**2) / (2.0 * WIDTH * WIDTH))
    g = np.cos(STEP * np.mod(np.outer(grid, grid), NG)) @ gauss
    circ = g[np.mod(grid[:, None] - grid[None, :], NG)]
    tables["circ"] = np.concatenate(parts(circ), axis=1)
    return tables


TABLES = build_tables()
NAMES = ("z_up", "y_up", "x_up", "py", "px", "circ", "pz", "piz", "pixp", "piy", "x_down", "y_down", "z_down", "pix")


def mm(a, b):
    return lax.dot_general(a, b, (((1,), (0,)), ((), ())), preferred_element_type=F32)


def mm_nt(a, b):
    return lax.dot_general(a, b, (((1,), (1,)), ((), ())), preferred_element_type=F32)


def split(x):
    hi = x.astype(BF16)
    return hi, (x - hi.astype(F32)).astype(BF16)


def stack_rows(x):
    hi, lo = split(x)
    return jnp.concatenate([hi, lo, hi], axis=0)


def stack_lanes(x):
    hi, lo = split(x)
    return jnp.concatenate([hi, lo, hi], axis=1)


def total(x):
    return jnp.sum(jnp.sum(x, axis=0, keepdims=True), axis=1, keepdims=True)


def iota(shape, axis):
    return lax.broadcasted_iota(jnp.int32, shape, axis)


def wrapped(x):
    return jnp.where(x < NG // 2, x, x - NG)


def turned(x):
    sgn = jnp.where(iota((1, 128), 1) < 64, 1.0, -1.0).astype(F32)
    return pltpu.roll(x, 64, 1) * sgn


def lanes_to_rows(x):
    return jnp.concatenate([x[:, i * 128 : (i + 1) * 128] for i in range(4)], axis=0)


def rows_to_lanes(x):
    return jnp.concatenate([x[i * 128 : (i + 1) * 128] for i in range(4)], axis=1)


def exponential_weights(first_energy, second_energy, spread):
    middle = 0.5 * (first_energy + second_energy)
    half_gap = 0.5 * (first_energy - second_energy)
    radius = jnp.sqrt(half_gap * half_gap + spread * spread)
    cosine = jnp.cos(TIME_STEP * radius)
    sine = jnp.sin(TIME_STEP * radius)
    along_first = sine * half_gap / radius
    along_second = sine * spread / radius
    phase_cos = jnp.cos(TIME_STEP * middle)
    phase_sin = jnp.sin(TIME_STEP * middle)
    weight_first = (
        phase_cos * cosine - phase_sin * along_first,
        -phase_cos * along_first - phase_sin * cosine,
    )
    weight_second = (-phase_sin * along_second, -phase_cos * along_second)
    return (weight_first, weight_second)


def kernel(coeffs_in, occ_in, cols_in, slots_in, atoms_in, *refs):
    t = dict(zip(NAMES, refs[: len(NAMES)]))
    held = dict(zip(NAMES, refs[-len(NAMES) - 1 : -1]))
    tsem = refs[-1]
    (new_out, dens_out, coeffs, occ, cols, slots, atoms, new, dens_val, sh, cz, kin, tt, mt, field, slv, cpad, apad, vloc, pot, wvec, sb1, rb1, xb, rsb, sbuf, tb, rb2,
     ub, rbv, dk, sb4, rb4, sb5, rb5, sbr, rbr, gz, ssem, rsem, isem, osem) = refs[len(NAMES) : -len(NAMES) - 1]
    me = lax.axis_index("pw")
    band = lax.axis_index("band")

    loads = {k: pltpu.make_async_copy(t[k], held[k], tsem.at[i]) for i, k in enumerate(NAMES)}
    inputs = (slots_in, slots), (coeffs_in, coeffs), (cols_in, cols), (occ_in, occ), (atoms_in, atoms)
    inputs = [pltpu.make_async_copy(a, b, isem.at[i]) for i, (a, b) in enumerate(inputs)]
    for copy in inputs:
        copy.start()

    def table(k):
        if k in loads:
            loads.pop(k).wait()
        return held[k][...]

    barrier = pltpu.get_barrier_semaphore()

    def greet_pw(i, carry):
        pl.semaphore_signal(barrier, inc=1, device_id={"pw": lax.rem(me + i, NP)}, device_id_type=MESH)
        return carry

    def greet_band(i, carry):
        pl.semaphore_signal(barrier, inc=1, device_id={"band": lax.rem(band + i, NB)}, device_id_type=MESH)
        return carry

    lax.fori_loop(1, NP, greet_pw, 0)
    lax.fori_loop(1, NB, greet_band, 0)
    for k in NAMES:
        loads[k].start()

    due = {}
    gone = {}

    def send_pw(src, dst, k):
        due[k], gone[k] = dst, dst.at[pl.ds(0, NP - 1)]
        pltpu.make_async_copy(src.at[me], dst.at[me], rsem.at[k]).start()

        def one(i, carry):
            to = lax.rem(me + i, NP)
            pltpu.make_async_remote_copy(
                src.at[to], dst.at[me], ssem.at[k], rsem.at[k], device_id={"pw": to}, device_id_type=MESH
            ).start()
            return carry

        lax.fori_loop(1, NP, one, 0)

    def send_band(src, dst, whole, k):
        due[k], gone[k] = whole, whole.at[pl.ds(0, whole.shape[0] // NB * (NB - 1))]
        pltpu.make_async_copy(src(band), dst, rsem.at[k]).start()

        def one(i, carry):
            to = lax.rem(band + i, NB)
            pltpu.make_async_remote_copy(
                src(to), dst, ssem.at[k], rsem.at[k], device_id={"band": to}, device_id_type=MESH
            ).start()
            return carry

        lax.fori_loop(1, NB, one, 0)

    def arrive(k):
        ref = due.pop(k)
        pltpu.make_async_copy(ref, ref, rsem.at[k]).wait()

    def finish():
        for k, ref in gone.items():
            pltpu.make_async_copy(ref, ref, ssem.at[k]).wait()

    inputs[0].wait()
    for i in range(NPW_DEV // 128):
        slv[:, i * 128 : (i + 1) * 128] = slots[i : i + 1]
    slot = slv[...]
    stick = lax.shift_right_logical(slot, 7)
    zval = lax.bitwise_and(slot, 127)
    kzi = lax.bitwise_and(zval + 32, 127)
    sh[...] = (iota((128, NPW_DEV), 0) == stick).astype(BF16)

    def scatter(re, im):
        hit = iota((KZ, NPW_DEV), 0) == kzi
        for c, x in enumerate((re, im)):
            hi = x.astype(BF16).astype(F32)
            lo = x - hi
            cz[c * KZ : (c + 1) * KZ] = jnp.where(hit, hi, 0.0).astype(BF16)
            cz[(2 + c) * KZ : (3 + c) * KZ] = jnp.where(hit, lo, 0.0).astype(BF16)
        g = mm_nt(cz[...], sh[...])
        g = g[: 2 * KZ] + g[2 * KZ :]
        return mm(table("z_up"), stack_rows(g)).reshape(NP, 8, 128)

    inputs[1].wait()
    sb1[0] = scatter(coeffs[0, 0:1], coeffs[1, 0:1])
    pl.semaphore_wait(barrier, NP - 1 + NB - 1)
    send_pw(sb1.at[0], rb1.at[0], A1)
    sb1[1] = scatter(coeffs[0, 1:2], coeffs[1, 1:2])
    send_pw(sb1.at[1], rb1.at[1], A1 + 1)

    inputs[2].wait()
    c0, c1, c2 = (cols[pl.ds(i, 8, stride=3), :] for i in range(3))
    lane8 = iota((8, 128), 1)
    blocks = (
        c0,
        jnp.where(lane8 < 32, pltpu.roll(c0, 32, 1), pltpu.roll(c1, 32, 1)),
        jnp.where(lane8 < 64, pltpu.roll(c1, 64, 1), pltpu.roll(c2, 64, 1)),
        pltpu.roll(c2, 96, 1),
    )
    for i, block in enumerate(blocks):
        cpad[pl.ds(i, 8, stride=4), :] = jnp.where(lane8 < ST, block, -1)
    c = cpad[...]
    xp = lax.bitwise_and(lax.shift_right_arithmetic(c, 7) + 32, 127)
    yp = lax.bitwise_and(c + 32, 127)
    edge = yp == 64
    r = jnp.where(edge, 16, lax.shift_right_logical(xp, 2))
    q = jnp.where(edge, 64, lax.bitwise_and(xp, 3) * 64 + yp)
    r = jnp.where(c < 0, -1, r)
    for p in range(NP):
        mt[:, p * 128 : (p + 1) * 128] = (iota((NR, 128), 0) == r[p : p + 1]).astype(F32)
        tt[:, p * 128 : (p + 1) * 128] = (iota((256, 128), 0) == q[p : p + 1]).astype(BF16)

    inputs[3].wait()
    inputs[4].wait()

    def to_field(rb):
        g = None
        for p0 in range(0, NP, 4):
            block = []
            for p in range(p0, p0 + 4):
                d = rb[p]
                m = mt[:, p * 128 : (p + 1) * 128]
                hi = d.astype(BF16).astype(F32)
                rows = [jnp.broadcast_to(v[i : i + 1], (NR, 128)) * m for v in (hi, d - hi) for i in range(8)]
                block.append(jnp.concatenate(rows, axis=0).astype(BF16))
            y = mm_nt(jnp.concatenate(block, axis=1), tt[:, p0 * 128 : (p0 + 4) * 128])
            g = y if g is None else g + y
        g = g[: 8 * NR] + g[8 * NR :]
        f = mm(stack_lanes(g), table("y_up"))
        re, im = [], []
        for z in range(4):
            a = f[(2 * z) * NR : (2 * z + 1) * NR]
            b = f[(2 * z + 1) * NR : (2 * z + 2) * NR]
            re.append(a[:, :512] - b[:, 512:])
            im.append(a[:, 512:] + b[:, :512])
        rows = [
            jnp.concatenate([x[z][:, j * 128 : (j + 1) * 128] for z in range(4)], axis=1)
            for x in (re, im)
            for j in range(4)
        ]
        return mm(table("x_up"), stack_rows(jnp.concatenate(rows, axis=0)))

    dens = None
    for n in range(2):
        arrive(A1 + n)
        f = to_field(rb1.at[n])
        field[n] = f
        term = (f[:128] * f[:128] + f[128:] * f[128:]) * (occ[n] * (1.0 / 16.0))
        dens = term if dens is None else dens + term

    def plane_x(x, name):
        flipped = jnp.concatenate([turned(x[:, z * 128 : (z + 1) * 128]) for z in range(4)], axis=1)
        return mm(table(name), stack_rows(jnp.concatenate([x, flipped], axis=0)))

    def plane_inverse(x, name):
        y = plane_x(x, name)
        return rows_to_lanes(mm(stack_lanes(lanes_to_rows(y)), table("piy")))

    means = []
    for z in range(4):
        means.append(total(dens[:, z * 128 : (z + 1) * 128]) * (1.0 / (NG * NG)))
    mean = jnp.concatenate([jnp.broadcast_to(m, (1, 128)) for m in means], axis=1)
    dens = dens - mean
    xb[...] = plane_x(rows_to_lanes(mm(stack_lanes(lanes_to_rows(dens)), table("py"))), "px")
    head = jnp.where(lax.bitwise_and(iota((8, 512), 1), 127) == 0, mean * float(NG * NG), 0.0)
    xb[0:8] = xb[0:8] + jnp.where(iota((8, 512), 0) == 0, head, 0.0)
    send_band(lambda to: xb.at[pl.ds(pl.multiple_of(16 * to, 16), 16)], rsb.at[band], rsb, RS)

    own = cpad[pl.ds(me, 1), :]
    wx = wrapped(lax.bitwise_and(lax.shift_right_arithmetic(own, 7), 127))
    wy = wrapped(lax.bitwise_and(own, 127))
    reach = wx * wx + wy * wy
    coarse = lax.shift_right_logical(reach, 5).astype(F32)
    fine = lax.bitwise_and(reach, 31).astype(F32)
    both = jnp.concatenate([jnp.broadcast_to(coarse, (8, 128)), jnp.broadcast_to(fine, (8, 128))], axis=0)
    picked = mm(both.astype(BF16), sh[...])
    wz = wrapped(zval)
    kin[...] = (123.4 / (NG * NG)) * (32.0 * picked[0:1] + picked[8:9] + (wz * wz).astype(F32))

    apad[...] = jnp.full((3, 1024), -1, jnp.int32)
    apad[:, : atoms.shape[1]] = atoms[...]

    def spots(row):
        hot = (iota((128, 1024), 0) == apad[row : row + 1]).astype(BF16)
        return mm(table("circ"), jnp.concatenate([hot, hot], axis=0))

    gz[...] = spots(2)
    gy_hi, gy_lo = split(spots(1))
    gx = spots(0) * FORM
    for z in range(4):
        gl = gx * gz[pl.ds(4 * me + z, 1), :]
        g_hi, g_lo = split(gl)
        vloc[:, z * 128 : (z + 1) * 128] = mm_nt(g_hi, gy_hi) + mm_nt(g_lo, gy_hi) + mm_nt(g_hi, gy_lo)

    row = iota((256, 128), 0)
    lane = iota((256, 128), 1)
    wkz = wrapped(lax.shift_right_logical(row, 1))
    kx = 16 * band + 2 * lax.div(me, 4) + lax.bitwise_and(row, 1)
    wkx = wrapped(kx)
    ky = lax.bitwise_and(lane, 63)
    q = wkz * wkz + wkx * wkx + ky * ky
    corner = jnp.logical_and(q == 0, lane == 64)
    q = jnp.where(corner, 4096, q).astype(F32)
    factor = jnp.where(q > 0.0, (HARTREE / NG**3) / jnp.maximum(q, 1.0), 0.0)

    arrive(RS)
    s = rsb[0]
    for i in range(1, NB):
        s = s + rsb[i]
    sbuf[...] = s
    for i in range(8):
        for z in range(4):
            tb[i, 2 * z : 2 * z + 2, :] = s[2 * i : 2 * i + 2, z * 128 : (z + 1) * 128]
    mine = lax.div(me, 4)
    pltpu.make_async_copy(tb.at[mine], rb2.at[me], rsem.at[A2]).start()

    def out_a2(i, carry):
        to = lax.rem(me + i, NP)
        pltpu.make_async_remote_copy(
            tb.at[lax.div(to, 4)], rb2.at[me], ssem.at[A2], rsem.at[A2], device_id={"pw": to}, device_id_type=MESH
        ).start()
        return carry

    lax.fori_loop(1, NP, out_a2, 0)
    due[A2], gone[A2] = rb2, rb2.at[pl.ds(0, NP - 1)]

    arrive(A2)
    x = rb2[...].reshape(256, 128)
    flat = jnp.logical_and(lane == 0, kx == 0)
    x = x - jnp.where(flat, jnp.sum(jnp.where(flat, x, 0.0), axis=0, keepdims=True) * (1.0 / NG), 0.0)
    x = mm(table("pz"), stack_rows(jnp.concatenate([x, turned(x)], axis=0))) * factor
    x = mm(table("piz"), stack_rows(jnp.concatenate([x, turned(x)], axis=0)))
    ub[...] = x.reshape(NP, 8, 128)
    low = lax.rem(me, 4)
    turn = band * 8 + mine
    place = pl.ds(pl.multiple_of(8 * turn, 8), 8)
    pltpu.make_async_copy(ub.at[me], rbv.at[place], rsem.at[A3]).start()

    def out_a3(i, carry):
        to = lax.rem(turn + i, 64)
        spot = 4 * lax.rem(to, 8) + low
        pltpu.make_async_remote_copy(
            ub.at[spot],
            rbv.at[place],
            ssem.at[A3],
            rsem.at[A3],
            device_id={"band": lax.div(to, 8), "pw": spot},
            device_id_type=MESH,
        ).start()
        return carry

    lax.fori_loop(1, 64, out_a3, 0)
    due[A3], gone[A3] = rbv, rbv.at[pl.ds(0, 8 * 63)]
    arrive(A3)
    vk = [
        jnp.concatenate([rbv[pl.ds(2 * z + k, 64, stride=8), :] for k in range(2)], axis=0) for z in range(4)
    ]
    pot[...] = plane_inverse(jnp.concatenate(vk, axis=1), "pixp") + vloc[...]

    lane1 = iota((8, 128), 1)
    weight = NPW / NG**3
    for n in range(2):
        f = field[n]
        v = pot[...]
        u = jnp.concatenate([v * f[:128], v * f[128:]], axis=0)
        nsq_part = total(coeffs[0, n : n + 1] * coeffs[0, n : n + 1] + coeffs[1, n : n + 1] * coeffs[1, n : n + 1])
        cross_part = weight * total(u[:128] * f[:128] + u[128:] * f[128:]) + total(
            kin[...]
            * (coeffs[0, n : n + 1] * coeffs[0, n : n + 1] + coeffs[1, n : n + 1] * coeffs[1, n : n + 1])
        )
        x = mm(table("x_down"), stack_rows(u))
        rows = [
            jnp.concatenate(
                [x[(c * 4 + j) * NR : (c * 4 + j + 1) * NR, z * 128 : (z + 1) * 128] for j in range(4)], axis=1
            )
            for z in range(4)
            for c in range(2)
        ]
        o = mm(stack_lanes(jnp.concatenate(rows, axis=0)), table("y_down"))
        rows = []
        for z in range(4):
            a = o[(2 * z) * NR : (2 * z + 1) * NR]
            b = o[(2 * z + 1) * NR : (2 * z + 2) * NR]
            rows.append(a[:, :256] + b[:, 256:])
            rows.append(b[:, :256] - a[:, 256:])
        hi, lo = split(jnp.concatenate(rows, axis=0))
        hilo = jnp.concatenate([hi, lo], axis=1)
        extra = jnp.where(lane1 == 96, nsq_part, 0.0) + jnp.where(lane1 == 97, cross_part, 0.0)

        hot = tt[...]
        y = mm(hilo, jnp.concatenate([hot, hot], axis=0))
        m = mt[...]
        y = jnp.concatenate(
            [jnp.sum(y[k * NR : (k + 1) * NR] * m, axis=0, keepdims=True) for k in range(8)], axis=0
        )
        for p in range(NP):
            sb4[n, p] = y[:, p * 128 : (p + 1) * 128] + extra
        send_pw(sb4.at[n], rb4.at[n], A4 + n)

    at_band = pl.ds(pl.multiple_of(16 * band, 16), 16)
    send_band(lambda to: sbuf, dk.at[at_band], dk, AGD)

    states = []
    for n in range(2):
        arrive(A4 + n)
        r = rb4[n]
        ends = jnp.sum(r, axis=0)[0:1]
        nsq = jnp.sum(jnp.where(iota((1, 128), 1) == 96, ends, 0.0), axis=1, keepdims=True) + EPSILON
        cross = jnp.sum(jnp.where(iota((1, 128), 1) == 97, ends, 0.0), axis=1, keepdims=True)
        alpha0 = cross / nsq
        g = mm(table("z_down"), stack_rows(r.reshape(256, 128)))
        hi, lo = split(g)
        hilo = jnp.concatenate([hi, lo], axis=1)

        hot = sh[...]
        y = mm(hilo, jnp.concatenate([hot, hot], axis=0))
        pick = iota((KZ, NPW_DEV), 0) == lax.bitwise_and(slv[...] + 32, 127)
        for c in range(2):
            part = jnp.sum(jnp.where(pick, y[c * KZ : (c + 1) * KZ], 0.0), axis=0, keepdims=True)
            wvec[n, c : c + 1] = part + (kin[...] - alpha0) * coeffs[c, n : n + 1]
        w_re = wvec[n, 0:1]
        w_im = wvec[n, 1:2]
        sb5[n] = scatter(w_re, w_im)
        send_pw(sb5.at[n], rb5.at[n], A5 + n)
        wsq = w_re * w_re + w_im * w_im
        states.append((nsq, alpha0, total(wsq), total(wsq * kin[...])))

    out = jnp.zeros((8, 128), F32)
    for n in range(2):
        arrive(A5 + n)
        f = to_field(rb5.at[n])
        energy = weight * total(pot[...] * (f[:128] * f[:128] + f[128:] * f[128:])) + states[n][3]
        out = out + jnp.where(lane1 == 2 * n, states[n][2], 0.0) + jnp.where(lane1 == 2 * n + 1, energy, 0.0)
    sbr[...] = out
    pltpu.make_async_copy(sbr, rbr.at[me], rsem.at[AR]).start()

    def out_ar(i, carry):
        to = lax.rem(me + i, NP)
        pltpu.make_async_remote_copy(
            sbr, rbr.at[me], ssem.at[AR], rsem.at[AR], device_id={"pw": to}, device_id_type=MESH
        ).start()
        return carry

    lax.fori_loop(1, NP, out_ar, 0)
    due[AR], gone[AR] = rbr, rbr.at[pl.ds(0, NP - 1)]
    arrive(AGD)
    d = plane_inverse(dk[...], "pix") * (1.0 / (NG * NG))
    for z in range(4):
        dens_val[z] = d[:, z * 128 : (z + 1) * 128]
    dens_copy = pltpu.make_async_copy(dens_val, dens_out, osem.at[0])
    dens_copy.start()
    arrive(AR)
    ends = jnp.sum(rbr[...], axis=0)[0:1]
    for n in range(2):
        nsq, alpha0 = states[n][0], states[n][1]
        ww = jnp.sum(jnp.where(iota((1, 128), 1) == 2 * n, ends, 0.0), axis=1, keepdims=True)
        ew = jnp.sum(jnp.where(iota((1, 128), 1) == 2 * n + 1, ends, 0.0), axis=1, keepdims=True)
        spread_sq = ww / nsq + EPSILON
        spread = jnp.sqrt(spread_sq)
        alpha1 = ew / (nsq * spread_sq)
        first, second = exponential_weights(alpha0, alpha1, spread)
        sec_re = second[0] / spread
        sec_im = second[1] / spread
        c_re, c_im = coeffs[0, n : n + 1], coeffs[1, n : n + 1]
        w_re, w_im = wvec[n, 0:1], wvec[n, 1:2]
        new[0, n : n + 1] = first[0] * c_re - first[1] * c_im + (sec_re * w_re - sec_im * w_im)
        new[1, n : n + 1] = first[0] * c_im + first[1] * c_re + (sec_re * w_im + sec_im * w_re)

    new_copy = pltpu.make_async_copy(new, new_out, osem.at[1])
    new_copy.start()
    finish()
    dens_copy.wait()
    new_copy.wait()


def copies(new_in, dens_in, new_out, dens_out):
    new_out[...] = new_in[...]
    dens_out[...] = dens_in[...]


def local(coeffs, occupation, stick_columns, sphere_slots, atom_sites):
    cols = stick_columns.reshape(NP * ST // 128, 128)
    slots = sphere_slots.reshape(NPW_DEV // 128, 128)
    hbm = pl.BlockSpec(memory_space=pl.ANY)
    vm = pl.BlockSpec(memory_space=pltpu.VMEM)
    tables = [jnp.asarray(TABLES[k]) for k in NAMES]
    V = pltpu.VMEM
    results = (
        jax.ShapeDtypeStruct((2, 2, NPW_DEV), F32),
        jax.ShapeDtypeStruct((4, NG, NG), F32),
    )
    step = pl.pallas_call(
        kernel,
        out_shape=results,
        in_specs=[hbm] * (5 + len(NAMES)),
        out_specs=(hbm, hbm),
        scratch_shapes=[
            V((2, 2, NPW_DEV), F32),
            pltpu.SMEM((2,), F32),
            V((NP * ST // 128, 128), jnp.int32),
            V((NPW_DEV // 128, 128), jnp.int32),
            V(atom_sites.shape, jnp.int32),
            V((2, 2, NPW_DEV), F32),
            V((4, NG, NG), F32),
            V((128, NPW_DEV), BF16),
            V((4 * KZ, NPW_DEV), BF16),
            V((1, NPW_DEV), F32),
            V((256, 4096), BF16),
            V((NR, 4096), F32),
            V((2, 256, 512), F32),
            V((1, NPW_DEV), jnp.int32),
            V((NP, 128), jnp.int32),
            V((3, 1024), jnp.int32),
            V((128, 512), F32),
            V((128, 512), F32),
            V((2, 2, NPW_DEV), F32),
            V((2, NP, 8, 128), F32),
            V((2, NP, 8, 128), F32),
            V((128, 512), F32),
            V((NB, 16, 512), F32),
            V((16, 512), F32),
            V((8, 8, 128), F32),
            V((NP, 8, 128), F32),
            V((NP, 8, 128), F32),
            V((512, 128), F32),
            V((128, 512), F32),
            V((2, NP, 8, 128), F32),
            V((2, NP, 8, 128), F32),
            V((2, NP, 8, 128), F32),
            V((2, NP, 8, 128), F32),
            V((8, 128), F32),
            V((NP, 8, 128), F32),
            V((128, 1024), F32),
            pltpu.SemaphoreType.DMA((N_SEM,)),
            pltpu.SemaphoreType.DMA((N_SEM,)),
            pltpu.SemaphoreType.DMA((5,)),
            pltpu.SemaphoreType.DMA((2,)),
        ]
        + [V(TABLES[k].shape, BF16) for k in NAMES]
        + [pltpu.SemaphoreType.DMA((len(NAMES),))],
        compiler_params=pltpu.CompilerParams(
            collective_id=0, has_side_effects=True, vmem_limit_bytes=60 * 1024 * 1024
        ),
        name="step",
    )(coeffs, occupation, cols, slots, atom_sites, *tables)
    return pl.pallas_call(
        copies,
        out_shape=results,
        in_specs=[vm, vm],
        out_specs=(vm, vm),
        name="results",
    )(*step)


def solution(mesh):
    in_specs = (P(None, "band", "pw"), P("band"), P(), P("pw"), P())
    out_specs = (P(None, "band", "pw"), P("pw", None, None))
    return jax.shard_map(local, mesh=mesh, in_specs=in_specs, out_specs=out_specs, check_vma=False)
```

```python
import functools
import math

import jax
import jax.numpy as jnp
import numpy as np
import ml_dtypes
from jax import lax
from jax.experimental import pallas as pl
from jax.experimental.pallas import tpu as pltpu
from jax.sharding import PartitionSpec as P

MESH = pl.DeviceIdType.MESH
F32 = jnp.float32
BF16 = jnp.bfloat16

NG = 128
NP = 32
NB = 8
NPW_DEV = 3584
NPW = NPW_DEV * NP
ST = 96
KH = 40
NR = 16
NX = 8 * NR + 16
TIME_STEP = 0.2
EPSILON = 1e-06
STEP = 2.0 * math.pi / NG
WIDTH = NG / 20.0
FORM = -2.0 / ((2.0 * math.pi) ** 1.5 * WIDTH**3)
TO_GRID = 1.0 / math.sqrt(NPW)
TO_SPHERE = math.sqrt(NPW) / NG**3
HARTREE = 0.1 * NG * NG

A1, RS, A2, A3, AGV, AGD, A4, A5, AR = 0, 2, 3, 4, 5, 6, 7, 9, 11
N_SEM = 12
MIX = 13
FAR_FIRST = (4, 3, 5, 2, 6, 1, 7)


def parts(x):
    hi = x.astype(np.float32).astype(ml_dtypes.bfloat16)
    lo = (x - hi.astype(np.float64)).astype(np.float32).astype(ml_dtypes.bfloat16)
    return hi, lo


def left_table(x):
    hi, lo = parts(x)
    return np.concatenate([hi, hi, lo], axis=1)


def right_table(x):
    hi, lo = parts(x)
    return np.concatenate([hi, hi, lo], axis=0)


def phases(rows, cols):
    angle = STEP * np.mod(np.outer(rows, cols), NG)
    return np.cos(angle), np.sin(angle)


def build_tables():
    grid = np.arange(NG)
    tables = {}
    kz = 2 * np.arange(KH)[None, :] + np.arange(2)[:, None]
    valid = (kz <= 64).reshape(-1).astype(np.float64)
    c, s = phases(grid, kz.reshape(-1) - 32)
    c, s = (c * valid).reshape(NG, 2, KH), (s * valid).reshape(NG, 2, KH)
    up = np.zeros((NG, 2, 2, 2, KH))
    up[:, 0, :, 0], up[:, 0, :, 1], up[:, 1, :, 0], up[:, 1, :, 1] = c, -s, s, c
    tables["z_up"] = left_table(up.reshape(2 * NG, 4 * KH))
    down = np.zeros((NG, 2, 2, 2, KH))
    down[:, 0, :, 0], down[:, 1, :, 0], down[:, 0, :, 1], down[:, 1, :, 1] = c, s, -s, c
    tables["z_down"] = left_table(down.reshape(2 * NG, 4 * KH).T)

    c, s = phases(np.arange(64) - 32, grid)
    hi, lo = parts(np.concatenate([c, s], axis=1))
    none = np.zeros_like(lo)
    tables["y_even"] = np.concatenate([hi, hi, lo, none])
    tables["y_odd"] = np.concatenate([hi, hi, none, lo])
    y_down = np.zeros((2, NG, 2, 2, 64))
    for j in range(2):
        y_down[j, :, 0, j], y_down[j, :, 1, j] = c.T, s.T
    tables["y_down"] = right_table(y_down.reshape(256, 256))

    wx = 4 * np.arange(NR)[None, :] + np.arange(4)[:, None] - 32
    c, s = phases(grid, wx.reshape(-1))
    x_up = np.zeros((2, NG, NX))
    x_up[:, :, : 8 * NR] = np.stack([np.concatenate([c, -s], axis=1), np.concatenate([s, c], axis=1)])
    for first, w in ((8 * NR, 32), (8 * NR + 2, 0)):
        c, s = phases(grid, np.array([w]))
        x_up[0, :, first], x_up[0, :, first + 1] = c[:, 0], -s[:, 0]
        x_up[1, :, first], x_up[1, :, first + 1] = s[:, 0], c[:, 0]
    tables["x_up"] = left_table(TO_GRID * x_up.reshape(2 * NG, NX))
    tables["x_down"] = left_table(TO_SPHERE * x_up.reshape(2 * NG, NX).T)

    c, s = phases(grid, np.arange(64))
    fwd = np.zeros((NG, 2, 64))
    fwd[:, 0], fwd[:, 1] = c, -s
    sign = np.where(grid % 2 == 0, 1.0, -1.0)
    fwd[:, 1, 0] = sign
    tables["py"] = right_table(fwd.reshape(NG, NG))
    inv = np.zeros((2, 64, NG))
    inv[0], inv[1] = 2.0 * c.T, -2.0 * s.T
    inv[0, 0], inv[1, 0] = 1.0, sign
    tables["piy"] = right_table(inv.reshape(NG, NG))
    c, s = phases(grid, grid)
    tables["px"] = left_table(np.concatenate([c, s], axis=1))
    tables["pix"] = left_table(np.concatenate([c, -s], axis=1))
    pairs = np.concatenate([grid[0::2], grid[1::2]])
    tables["pixp"] = left_table(np.concatenate([c[:, pairs], -s[:, pairs]], axis=1))
    order = (4 * np.arange(NP)[None, :] + np.arange(4)[:, None]).reshape(-1)
    tables["pz"] = left_table(np.concatenate([c[:, order], s[:, order]], axis=1))
    tables["piz"] = left_table(np.concatenate([c[order], -s[order]], axis=1))

    wk = np.where(grid < 64, grid, grid - NG)
    gauss = np.exp(-(wk**2) / (2.0 * WIDTH * WIDTH))
    g = np.cos(STEP * np.mod(np.outer(grid, grid), NG)) @ gauss
    circ = g[np.mod(grid[:, None] - grid[None, :], NG)]
    tables["circ"] = np.concatenate(parts(circ), axis=1)
    return tables


TABLES = build_tables()
NAMES = ("z_up", "y_even", "y_odd", "x_up", "py", "px", "circ", "pz", "piz", "pixp", "piy", "x_down", "y_down", "z_down", "pix")


def mm(a, b):
    return lax.dot_general(a, b, (((1,), (0,)), ((), ())), preferred_element_type=F32)


def mm_nt(a, b):
    return lax.dot_general(a, b, (((1,), (1,)), ((), ())), preferred_element_type=F32)


def split(x):
    hi = x.astype(BF16)
    return hi, (x - hi.astype(F32)).astype(BF16)


def stack_rows(x):
    hi, lo = split(x)
    return jnp.concatenate([hi, lo, hi], axis=0)


def stack_lanes(x):
    hi, lo = split(x)
    return jnp.concatenate([hi, lo, hi], axis=1)


def total(x):
    return jnp.sum(jnp.sum(x, axis=0, keepdims=True), axis=1, keepdims=True)


def iota(shape, axis):
    return lax.broadcasted_iota(jnp.int32, shape, axis)


def wrapped(x):
    return jnp.where(x < NG // 2, x, x - NG)


def turned(x):
    sgn = jnp.where(iota((1, 128), 1) < 64, 1.0, -1.0).astype(F32)
    blocks = [pltpu.roll(x[:, i : i + 128], 64, 1) * sgn for i in range(0, x.shape[1], 128)]
    return jnp.concatenate(blocks, axis=1)


def lanes_to_rows(x):
    return jnp.concatenate([x[:, i * 128 : (i + 1) * 128] for i in range(4)], axis=0)


def rows_to_lanes(x):
    return jnp.concatenate([x[i * 128 : (i + 1) * 128] for i in range(4)], axis=1)


def exponential_weights(first_energy, second_energy, spread):
    middle = 0.5 * (first_energy + second_energy)
    half_gap = 0.5 * (first_energy - second_energy)
    radius = jnp.sqrt(half_gap * half_gap + spread * spread)
    cosine = jnp.cos(TIME_STEP * radius)
    sine = jnp.sin(TIME_STEP * radius)
    along_first = sine * half_gap / radius
    along_second = sine * spread / radius
    phase_cos = jnp.cos(TIME_STEP * middle)
    phase_sin = jnp.sin(TIME_STEP * middle)
    weight_first = (
        phase_cos * cosine - phase_sin * along_first,
        -phase_cos * along_first - phase_sin * cosine,
    )
    weight_second = (-phase_sin * along_second, -phase_cos * along_second)
    return (weight_first, weight_second)


def kernel(coeffs_in, occ_in, cols_in, slots_in, atoms_in, *refs):
    t = dict(zip(NAMES, refs[: len(NAMES)]))
    held = dict(zip(NAMES, refs[-len(NAMES) - 1 : -1]))
    tsem = refs[-1]
    (new_out, dens_out, coeffs, occ, cols, slots, atoms, new, dens_val, sh, sht, cz, kin, tt, mt, ms, field, slv, cpad, apad, vloc, pot, wvec, sb1, rb1, xb, rsb, sbuf, tb, rb2,
     ub, rbv, dk, sb4, rb4, sb5, rb5, sbr, rbr, gz, ssem, rsem, isem, osem) = refs[len(NAMES) : -len(NAMES) - 1]
    me = lax.axis_index("pw")
    band = lax.axis_index("band")

    loads = {k: pltpu.make_async_copy(t[k], held[k], tsem.at[i]) for i, k in enumerate(NAMES)}
    inputs = (slots_in, slots), (coeffs_in, coeffs), (cols_in, cols), (occ_in, occ), (atoms_in, atoms)
    inputs = [pltpu.make_async_copy(a, b, isem.at[i]) for i, (a, b) in enumerate(inputs)]
    for copy in inputs:
        copy.start()

    def table(k):
        if k in loads:
            loads.pop(k).wait()
        return held[k][...]

    barrier = pltpu.get_barrier_semaphore()

    def greet_pw(i, carry):
        pl.semaphore_signal(barrier, inc=1, device_id={"pw": lax.rem(me + i, NP)}, device_id_type=MESH)
        return carry

    def greet_band(i, carry):
        pl.semaphore_signal(barrier, inc=1, device_id={"band": lax.rem(band + i, NB)}, device_id_type=MESH)
        return carry

    lax.fori_loop(1, NP, greet_pw, 0)
    lax.fori_loop(1, NB, greet_band, 0)
    for k in NAMES:
        loads[k].start()

    due = {}
    gone = {}

    def send_pw(src, dst, k):
        due[k], gone[k] = dst, dst.at[pl.ds(0, NP - 1)]
        pltpu.make_async_copy(src.at[me], dst.at[me], rsem.at[k]).start()

        def one(i, carry):
            to = lax.rem(me + MIX * i, NP)
            pltpu.make_async_remote_copy(
                src.at[to], dst.at[me], ssem.at[k], rsem.at[k], device_id={"pw": to}, device_id_type=MESH
            ).start()
            return carry

        lax.fori_loop(1, NP, one, 0)

    def send_band(src, dst, whole, k):
        due[k], gone[k] = whole, whole.at[pl.ds(0, whole.shape[0] // NB * (NB - 1))]
        pltpu.make_async_copy(src(band), dst, rsem.at[k]).start()

        for i in FAR_FIRST:
            to = lax.rem(band + i, NB)
            pltpu.make_async_remote_copy(
                src(to), dst, ssem.at[k], rsem.at[k], device_id={"band": to}, device_id_type=MESH
            ).start()

    def arrive(k):
        ref = due.pop(k)
        pltpu.make_async_copy(ref, ref, rsem.at[k]).wait()

    def finish():
        for k, ref in gone.items():
            pltpu.make_async_copy(ref, ref, ssem.at[k]).wait()

    inputs[0].wait()
    for i in range(NPW_DEV // 128):
        slv[:, i * 128 : (i + 1) * 128] = slots[i : i + 1]
    slot = slv[...]
    stick = lax.shift_right_logical(slot, 7)
    zval = lax.bitwise_and(slot, 127)
    kzi = lax.bitwise_and(zval + 32, 127)
    khi = lax.shift_right_logical(kzi, 1)
    sh[...] = (iota((256, NPW_DEV), 0) == lax.bitwise_and(kzi, 1) * 128 + stick).astype(BF16)

    def scatter(re, im, late):
        hit = iota((KH, NPW_DEV), 0) == khi
        re_hi = re.astype(BF16).astype(F32)
        im_hi = im.astype(BF16).astype(F32)
        for k, pair in enumerate(((re_hi, im_hi), (re - re_hi, im - im_hi))):
            rows = jnp.concatenate([jnp.where(hit, x, 0.0) for x in pair], axis=0)
            cz[k * 2 * KH : (k + 1) * 2 * KH] = rows.astype(BF16)
        g = mm(cz[...], sht[...]) if late else mm_nt(cz[...], sh[...])
        g = g[: 2 * KH] + g[2 * KH :]
        g = jnp.concatenate([g[:, :128], g[:, 128:]], axis=0)
        return mm(table("z_up"), stack_rows(g)).reshape(NP, 8, 128)

    inputs[1].wait()
    sb1[0] = scatter(coeffs[0, 0:1], coeffs[1, 0:1], False)
    pl.semaphore_wait(barrier, NP - 1 + NB - 1)
    send_pw(sb1.at[0], rb1.at[0], A1)
    sb1[1] = scatter(coeffs[0, 1:2], coeffs[1, 1:2], False)
    send_pw(sb1.at[1], rb1.at[1], A1 + 1)

    inputs[2].wait()
    c0, c1, c2 = (cols[pl.ds(i, 8, stride=3), :] for i in range(3))
    lane8 = iota((8, 128), 1)
    blocks = (
        c0,
        jnp.where(lane8 < 32, pltpu.roll(c0, 32, 1), pltpu.roll(c1, 32, 1)),
        jnp.where(lane8 < 64, pltpu.roll(c1, 64, 1), pltpu.roll(c2, 64, 1)),
        pltpu.roll(c2, 96, 1),
    )
    for i, block in enumerate(blocks):
        cpad[pl.ds(i, 8, stride=4), :] = jnp.where(lane8 < ST, block, -1)
    c = cpad[...]
    xp = lax.bitwise_and(lax.shift_right_arithmetic(c, 7) + 32, 127)
    yp = lax.bitwise_and(c + 32, 127)
    far_x = jnp.logical_and(c >= 0, xp == 64)
    far_y = jnp.logical_and(c >= 0, yp == 64)
    regular = jnp.logical_and(c >= 0, jnp.logical_and(xp < 64, yp < 64))
    r = jnp.where(regular, lax.shift_right_logical(xp, 2), -1)
    q = lax.bitwise_and(xp, 3) * 64 + yp
    for p in range(NP):
        at = slice(p * 128, (p + 1) * 128)
        mt[:, at] = (iota((NR, 128), 0) == r[p : p + 1]).astype(F32)
        tt[:, at] = (iota((256, 128), 0) == q[p : p + 1]).astype(BF16)
        ms[0:1, at] = far_x[p : p + 1].astype(F32)
        ms[1:2, at] = far_y[p : p + 1].astype(F32)

    inputs[3].wait()
    inputs[4].wait()

    quarter = lax.bitwise_and(iota((1, 128), 1), 3)
    cos_b = jnp.where(quarter == 0, 1.0, jnp.where(quarter == 2, -1.0, 0.0))
    sin_b = jnp.where(quarter == 1, 1.0, jnp.where(quarter == 3, -1.0, 0.0))

    def to_field(rb):
        g = None
        ends = [jnp.zeros((8, 128), F32), jnp.zeros((8, 128), F32)]
        for p0 in range(0, NP, 4):
            block = []
            for p in range(p0, p0 + 4):
                d = rb[p]
                m = mt[:, p * 128 : (p + 1) * 128]
                ends = [x + d * ms[i : i + 1, p * 128 : (p + 1) * 128] for i, x in enumerate(ends)]
                hi = d.astype(BF16).astype(F32)
                rows = [jnp.broadcast_to(v[i : i + 1], (NR, 128)) * m for v in (hi, d - hi) for i in range(8)]
                block.append(jnp.concatenate(rows, axis=0).astype(BF16))
            y = mm_nt(jnp.concatenate(block, axis=1), tt[:, p0 * 128 : (p0 + 4) * 128])
            g = y if g is None else g + y
        g = g[: 8 * NR] + g[8 * NR :]
        hi = g.astype(BF16).astype(F32)
        lo = g - hi
        left = iota((1, 128), 1) < 64
        re, im = [], []
        for j in range(4):
            at = slice(j // 2 * 128, j // 2 * 128 + 128)
            h, l = hi[:, at], pltpu.roll(lo[:, at], 64, 1)
            both = jnp.where(left, h, l) if j % 2 == 0 else jnp.where(left, l, h)
            f = jnp.concatenate([both, h], axis=1).astype(BF16)
            f = mm(f, table("y_even" if j % 2 == 0 else "y_odd"))
            row_re, row_im = [], []
            for z in range(4):
                a = f[(2 * z) * NR : (2 * z + 1) * NR]
                b = f[(2 * z + 1) * NR : (2 * z + 2) * NR]
                row_re.append(a[:, :128] - b[:, 128:])
                row_im.append(a[:, 128:] + b[:, :128])
            re.append(jnp.concatenate(row_re, axis=1))
            im.append(jnp.concatenate(row_im, axis=1))
        rows = re + im
        ex, ey = (jnp.sum(x, axis=1, keepdims=True) for x in ends)
        extra = []
        for z in range(4):
            k = 2 * z
            yr, yi = ey[k : k + 1], ey[k + 1 : k + 2]
            x = jnp.broadcast_to(ex[k : k + 2], (2, 128))
            y = [yr * cos_b - yi * sin_b, yr * sin_b + yi * cos_b]
            extra.append(jnp.concatenate([x] + y + [jnp.zeros((12, 128), F32)], axis=0))
        rows.append(jnp.concatenate(extra, axis=1))
        return mm(table("x_up"), stack_rows(jnp.concatenate(rows, axis=0)))

    dens = None
    for n in range(2):
        arrive(A1 + n)
        f = to_field(rb1.at[n])
        field[n] = f
        term = (f[:128] * f[:128] + f[128:] * f[128:]) * (occ[n] * (1.0 / 16.0))
        dens = term if dens is None else dens + term

    def plane_x(x, name):
        flipped = jnp.concatenate([turned(x[:, z * 128 : (z + 1) * 128]) for z in range(4)], axis=1)
        return mm(table(name), stack_rows(jnp.concatenate([x, flipped], axis=0)))

    def plane_inverse(x, name):
        y = plane_x(x, name)
        return rows_to_lanes(mm(stack_lanes(lanes_to_rows(y)), table("piy")))

    means = []
    for z in range(4):
        means.append(total(dens[:, z * 128 : (z + 1) * 128]) * (1.0 / (NG * NG)))
    mean = jnp.concatenate([jnp.broadcast_to(m, (1, 128)) for m in means], axis=1)
    dens = dens - mean
    xb[...] = plane_x(rows_to_lanes(mm(stack_lanes(lanes_to_rows(dens)), table("py"))), "px")
    head = jnp.where(lax.bitwise_and(iota((8, 512), 1), 127) == 0, mean * float(NG * NG), 0.0)
    xb[0:8] = xb[0:8] + jnp.where(iota((8, 512), 0) == 0, head, 0.0)
    send_band(lambda to: xb.at[pl.ds(pl.multiple_of(16 * to, 16), 16)], rsb.at[band], rsb, RS)

    own = cpad[pl.ds(me, 1), :]
    wx = wrapped(lax.bitwise_and(lax.shift_right_arithmetic(own, 7), 127))
    wy = wrapped(lax.bitwise_and(own, 127))
    reach = wx * wx + wy * wy
    coarse = lax.shift_right_logical(reach, 5).astype(F32)
    fine = lax.bitwise_and(reach, 31).astype(F32)
    both = jnp.concatenate([jnp.broadcast_to(coarse, (8, 128)), jnp.broadcast_to(fine, (8, 128))], axis=0)
    picked = mm(jnp.concatenate([both, both], axis=1).astype(BF16), sh[...])
    wz = wrapped(zval)
    kin[...] = (123.4 / (NG * NG)) * (32.0 * picked[0:1] + picked[8:9] + (wz * wz).astype(F32))

    apad[...] = jnp.full((3, 1024), -1, jnp.int32)
    apad[:, : atoms.shape[1]] = atoms[...]

    def spots(row):
        hot = (iota((128, 1024), 0) == apad[row : row + 1]).astype(BF16)
        return mm(table("circ"), jnp.concatenate([hot, hot], axis=0))

    gz[...] = spots(2)
    gy_hi, gy_lo = split(spots(1))
    gx = spots(0) * FORM
    for z in range(4):
        gl = gx * gz[pl.ds(4 * me + z, 1), :]
        g_hi, g_lo = split(gl)
        vloc[:, z * 128 : (z + 1) * 128] = mm_nt(g_hi, gy_hi) + mm_nt(g_lo, gy_hi) + mm_nt(g_hi, gy_lo)

    lane = iota((128, 256), 1)
    wkz = wrapped(iota((128, 256), 0))
    kx = 16 * band + 2 * lax.div(me, 4) + lax.shift_right_logical(lane, 7)
    lane = lax.bitwise_and(lane, 127)
    wkx = wrapped(kx)
    ky = lax.bitwise_and(lane, 63)
    q = wkz * wkz + wkx * wkx + ky * ky
    corner = jnp.logical_and(q == 0, lane == 64)
    q = jnp.where(corner, 4096, q).astype(F32)
    factor = jnp.where(q > 0.0, (HARTREE / NG**3) / jnp.maximum(q, 1.0), 0.0)

    def transpose(i, carry):
        at = pl.ds(pl.multiple_of(i * 512, 512), 512)
        sht[at, :] = sh[:, at].T
        return carry

    lax.fori_loop(0, NPW_DEV // 512, transpose, 0)
    arrive(RS)
    s = rsb[0]
    for i in range(1, NB):
        s = s + rsb[i]
    sbuf[...] = s
    for i in range(8):
        for z in range(4):
            tb[i, 2 * z : 2 * z + 2, :] = s[2 * i : 2 * i + 2, z * 128 : (z + 1) * 128]
    mine = lax.div(me, 4)
    slot_me = pl.ds(pl.multiple_of(8 * me, 8), 8)
    pltpu.make_async_copy(tb.at[mine], rb2.at[slot_me], rsem.at[A2]).start()

    def out_a2(i, carry):
        to = lax.rem(me + MIX * i, NP)
        pltpu.make_async_remote_copy(
            tb.at[lax.div(to, 4)], rb2.at[slot_me], ssem.at[A2], rsem.at[A2], device_id={"pw": to}, device_id_type=MESH
        ).start()
        return carry

    lax.fori_loop(1, NP, out_a2, 0)
    due[A2], gone[A2] = rb2, rb2.at[pl.ds(0, 8 * (NP - 1))]

    arrive(A2)
    x = [
        jnp.concatenate([rb2[pl.ds(2 * z + k, NP, stride=8), :] for z in range(4)], axis=0) for k in range(2)
    ]
    x = jnp.concatenate(x, axis=1)
    flat = jnp.logical_and(lane == 0, kx == 0)
    x = x - jnp.where(flat, jnp.sum(jnp.where(flat, x, 0.0), axis=0, keepdims=True) * (1.0 / NG), 0.0)
    x = mm(table("pz"), stack_rows(jnp.concatenate([x, turned(x)], axis=0))) * factor
    x = mm(table("piz"), stack_rows(jnp.concatenate([x, turned(x)], axis=0)))
    for z in range(4):
        for k in range(2):
            ub[pl.ds(2 * z + k, NP, stride=8), :] = x[z * NP : (z + 1) * NP, k * 128 : (k + 1) * 128]
    low = lax.rem(me, 4)
    turn = band * 8 + mine
    place = pl.ds(pl.multiple_of(8 * turn, 8), 8)
    pltpu.make_async_copy(ub.at[slot_me], rbv.at[place], rsem.at[A3]).start()

    def out_a3(i, offsets):
        spot = 4 * lax.rem(mine + i, 8) + low
        for offset in offsets:
            pltpu.make_async_remote_copy(
                ub.at[pl.ds(pl.multiple_of(8 * spot, 8), 8)],
                rbv.at[place],
                ssem.at[A3],
                rsem.at[A3],
                device_id={"band": lax.rem(band + offset, NB), "pw": spot},
                device_id_type=MESH,
            ).start()

    def out_far(i, carry):
        out_a3(i, FAR_FIRST)
        return carry

    def out_near(i, carry):
        out_a3(i, (0,))
        return carry

    lax.fori_loop(0, 8, out_far, 0)
    lax.fori_loop(1, 8, out_near, 0)
    due[A3], gone[A3] = rbv, rbv.at[pl.ds(0, 8 * 63)]
    arrive(A3)
    vk = [
        jnp.concatenate([rbv[pl.ds(2 * z + k, 64, stride=8), :] for k in range(2)], axis=0) for z in range(4)
    ]
    pot[...] = plane_inverse(jnp.concatenate(vk, axis=1), "pixp") + vloc[...]

    lane1 = iota((8, 128), 1)
    weight = NPW / NG**3
    for n in range(2):
        f = field[n]
        v = pot[...]
        u = jnp.concatenate([v * f[:128], v * f[128:]], axis=0)
        nsq_part = total(coeffs[0, n : n + 1] * coeffs[0, n : n + 1] + coeffs[1, n : n + 1] * coeffs[1, n : n + 1])
        cross_part = weight * total(u[:128] * f[:128] + u[128:] * f[128:]) + total(
            kin[...]
            * (coeffs[0, n : n + 1] * coeffs[0, n : n + 1] + coeffs[1, n : n + 1] * coeffs[1, n : n + 1])
        )
        x = mm(table("x_down"), stack_rows(u))
        tiles = []
        for t in range(2):
            rows = [
                jnp.concatenate(
                    [x[(c * 4 + j) * NR : (c * 4 + j + 1) * NR, z * 128 : (z + 1) * 128] for j in (2 * t, 2 * t + 1)],
                    axis=1,
                )
                for z in range(4)
                for c in range(2)
            ]
            o = mm(stack_lanes(jnp.concatenate(rows, axis=0)), table("y_down"))
            rows = []
            for z in range(4):
                a = o[(2 * z) * NR : (2 * z + 1) * NR]
                b = o[(2 * z + 1) * NR : (2 * z + 2) * NR]
                rows.append(a[:, :128] + b[:, 128:])
                rows.append(b[:, :128] - a[:, 128:])
            tiles.append(jnp.concatenate(rows, axis=0))
        hi, lo = split(jnp.concatenate(tiles, axis=1))
        edge = x[8 * NR :]
        ex, ey = [], []
        for z in range(4):
            a, b, c, d = (edge[i : i + 1, z * 128 : (z + 1) * 128] for i in range(4))
            ex += [a, b]
            ey += [c * cos_b + d * sin_b, d * cos_b - c * sin_b]
        ex, ey = (jnp.sum(jnp.concatenate(v, axis=0), axis=1, keepdims=True) for v in (ex, ey))
        extra = jnp.where(lane1 == 96, nsq_part, 0.0) + jnp.where(lane1 == 97, cross_part, 0.0)

        y = mm(jnp.concatenate([hi, lo], axis=0), tt[...])
        y = y[: 8 * NR] + y[8 * NR :]
        m = mt[...]
        y = jnp.concatenate(
            [jnp.sum(y[k * NR : (k + 1) * NR] * m, axis=0, keepdims=True) for k in range(8)], axis=0
        )
        y = y + ex * ms[0:1] + ey * ms[1:2]
        for p in range(NP):
            sb4[n, p] = y[:, p * 128 : (p + 1) * 128] + extra
        send_pw(sb4.at[n], rb4.at[n], A4 + n)

    at_band = pl.ds(pl.multiple_of(16 * band, 16), 16)
    send_band(lambda to: sbuf, dk.at[at_band], dk, AGD)

    states = []
    for n in range(2):
        arrive(A4 + n)
        r = rb4[n]
        ends = jnp.sum(r, axis=0)[0:1]
        nsq = jnp.sum(jnp.where(iota((1, 128), 1) == 96, ends, 0.0), axis=1, keepdims=True) + EPSILON
        cross = jnp.sum(jnp.where(iota((1, 128), 1) == 97, ends, 0.0), axis=1, keepdims=True)
        alpha0 = cross / nsq
        g = mm(table("z_down"), stack_rows(r.reshape(256, 128)))
        hi, lo = split(jnp.concatenate([g[: 2 * KH], g[2 * KH :]], axis=1))
        y = mm(jnp.concatenate([hi, lo], axis=0), sh[...])
        y = y[: 2 * KH] + y[2 * KH :]
        pick = iota((KH, NPW_DEV), 0) == khi
        for c in range(2):
            part = jnp.sum(jnp.where(pick, y[c * KH : (c + 1) * KH], 0.0), axis=0, keepdims=True)
            wvec[n, c : c + 1] = part + (kin[...] - alpha0) * coeffs[c, n : n + 1]
        w_re = wvec[n, 0:1]
        w_im = wvec[n, 1:2]
        sb5[n] = scatter(w_re, w_im, True)
        send_pw(sb5.at[n], rb5.at[n], A5 + n)
        wsq = w_re * w_re + w_im * w_im
        states.append((nsq, alpha0, total(wsq), total(wsq * kin[...])))

    out = jnp.zeros((8, 128), F32)
    for n in range(2):
        arrive(A5 + n)
        f = to_field(rb5.at[n])
        energy = weight * total(pot[...] * (f[:128] * f[:128] + f[128:] * f[128:])) + states[n][3]
        out = out + jnp.where(lane1 == 2 * n, states[n][2], 0.0) + jnp.where(lane1 == 2 * n + 1, energy, 0.0)
    sbr[...] = out
    pltpu.make_async_copy(sbr, rbr.at[me], rsem.at[AR]).start()

    def out_ar(i, carry):
        to = lax.rem(me + i, NP)
        pltpu.make_async_remote_copy(
            sbr, rbr.at[me], ssem.at[AR], rsem.at[AR], device_id={"pw": to}, device_id_type=MESH
        ).start()
        return carry

    lax.fori_loop(1, NP, out_ar, 0)
    due[AR], gone[AR] = rbr, rbr.at[pl.ds(0, NP - 1)]
    arrive(AGD)
    d = plane_inverse(dk[...], "pix") * (1.0 / (NG * NG))
    for z in range(4):
        dens_val[z] = d[:, z * 128 : (z + 1) * 128]
    dens_copy = pltpu.make_async_copy(dens_val, dens_out, osem.at[0])
    dens_copy.start()
    arrive(AR)
    ends = jnp.sum(rbr[...], axis=0)[0:1]
    for n in range(2):
        nsq, alpha0 = states[n][0], states[n][1]
        ww = jnp.sum(jnp.where(iota((1, 128), 1) == 2 * n, ends, 0.0), axis=1, keepdims=True)
        ew = jnp.sum(jnp.where(iota((1, 128), 1) == 2 * n + 1, ends, 0.0), axis=1, keepdims=True)
        spread_sq = ww / nsq + EPSILON
        spread = jnp.sqrt(spread_sq)
        alpha1 = ew / (nsq * spread_sq)
        first, second = exponential_weights(alpha0, alpha1, spread)
        sec_re = second[0] / spread
        sec_im = second[1] / spread
        c_re, c_im = coeffs[0, n : n + 1], coeffs[1, n : n + 1]
        w_re, w_im = wvec[n, 0:1], wvec[n, 1:2]
        new[0, n : n + 1] = first[0] * c_re - first[1] * c_im + (sec_re * w_re - sec_im * w_im)
        new[1, n : n + 1] = first[0] * c_im + first[1] * c_re + (sec_re * w_im + sec_im * w_re)

    new_copy = pltpu.make_async_copy(new, new_out, osem.at[1])
    new_copy.start()
    finish()
    dens_copy.wait()
    new_copy.wait()


def copies(new_in, dens_in, new_out, dens_out):
    new_out[...] = new_in[...]
    dens_out[...] = dens_in[...]


def local(coeffs, occupation, stick_columns, sphere_slots, atom_sites):
    cols = stick_columns.reshape(NP * ST // 128, 128)
    slots = sphere_slots.reshape(NPW_DEV // 128, 128)
    hbm = pl.BlockSpec(memory_space=pl.ANY)
    vm = pl.BlockSpec(memory_space=pltpu.VMEM)
    tables = [jnp.asarray(TABLES[k]) for k in NAMES]
    V = pltpu.VMEM
    results = (
        jax.ShapeDtypeStruct((2, 2, NPW_DEV), F32),
        jax.ShapeDtypeStruct((4, NG, NG), F32),
    )
    step = pl.pallas_call(
        kernel,
        out_shape=results,
        in_specs=[hbm] * (5 + len(NAMES)),
        out_specs=(hbm, hbm),
        scratch_shapes=[
            V((2, 2, NPW_DEV), F32),
            pltpu.SMEM((2,), F32),
            V((NP * ST // 128, 128), jnp.int32),
            V((NPW_DEV // 128, 128), jnp.int32),
            V(atom_sites.shape, jnp.int32),
            V((2, 2, NPW_DEV), F32),
            V((4, NG, NG), F32),
            V((256, NPW_DEV), BF16),
            V((NPW_DEV, 256), BF16),
            V((4 * KH, NPW_DEV), BF16),
            V((1, NPW_DEV), F32),
            V((256, 4096), BF16),
            V((NR, 4096), F32),
            V((2, 4096), F32),
            V((2, 256, 512), F32),
            V((1, NPW_DEV), jnp.int32),
            V((NP, 128), jnp.int32),
            V((3, 1024), jnp.int32),
            V((128, 512), F32),
            V((128, 512), F32),
            V((2, 2, NPW_DEV), F32),
            V((2, NP, 8, 128), F32),
            V((2, NP, 8, 128), F32),
            V((128, 512), F32),
            V((NB, 16, 512), F32),
            V((16, 512), F32),
            V((8, 8, 128), F32),
            V((8 * NP, 128), F32),
            V((8 * NP, 128), F32),
            V((512, 128), F32),
            V((128, 512), F32),
            V((2, NP, 8, 128), F32),
            V((2, NP, 8, 128), F32),
            V((2, NP, 8, 128), F32),
            V((2, NP, 8, 128), F32),
            V((8, 128), F32),
            V((NP, 8, 128), F32),
            V((128, 1024), F32),
            pltpu.SemaphoreType.DMA((N_SEM,)),
            pltpu.SemaphoreType.DMA((N_SEM,)),
            pltpu.SemaphoreType.DMA((5,)),
            pltpu.SemaphoreType.DMA((2,)),
        ]
        + [V(TABLES[k].shape, BF16) for k in NAMES]
        + [pltpu.SemaphoreType.DMA((len(NAMES),))],
        compiler_params=pltpu.CompilerParams(
            collective_id=0, has_side_effects=True, vmem_limit_bytes=60 * 1024 * 1024
        ),
        name="step",
    )(coeffs, occupation, cols, slots, atom_sites, *tables)
    return pl.pallas_call(
        copies,
        out_shape=results,
        in_specs=[vm, vm],
        out_specs=(vm, vm),
        name="results",
    )(*step)


def solution(mesh):
    in_specs = (P(None, "band", "pw"), P("band"), P(), P("pw"), P())
    out_specs = (P(None, "band", "pw"), P("pw", None, None))
    return jax.shard_map(local, mesh=mesh, in_specs=in_specs, out_specs=out_specs, check_vma=False)
```

```python
import functools
import math

import jax
import jax.numpy as jnp
import numpy as np
import ml_dtypes
from jax import lax
from jax.experimental import pallas as pl
from jax.experimental.pallas import tpu as pltpu
from jax.sharding import PartitionSpec as P

MESH = pl.DeviceIdType.MESH
F32 = jnp.float32
BF16 = jnp.bfloat16

NG = 128
NP = 32
NB = 8
NPW_DEV = 3584
NPW = NPW_DEV * NP
ST = 96
KH = 40
NR = 16
NQ = NP * ST // 128
NX = 8 * NR + 16
TIME_STEP = 0.2
EPSILON = 1e-06
STEP = 2.0 * math.pi / NG
WIDTH = NG / 20.0
FORM = -2.0 / ((2.0 * math.pi) ** 1.5 * WIDTH**3)
TO_GRID = 1.0 / math.sqrt(NPW)
TO_SPHERE = math.sqrt(NPW) / NG**3
HARTREE = 0.1 * NG * NG

A1, RS, A2, A3, AGV, AGD, A4, A5, AR = 0, 2, 3, 4, 5, 6, 7, 9, 11
N_SEM = 12
PEERS = tuple(sorted(((x, y, c) for x in range(4) for y in range(4) for c in (0, 1) if x or y or c), key=lambda d: (-min(d[0], 4 - d[0]) - min(d[1], 4 - d[1]), (d[0] + 3 * d[1]) % 4, d[2])))
FAR_FIRST = (4, 3, 5, 2, 6, 1, 7)
TARGETS = tuple(
    sorted(
        ((b, x, h) for x in (2, 1, 3, 0) for h in (1, 0) for b in FAR_FIRST + (0,) if b or x or h),
        key=lambda d: -min(d[0], 8 - d[0]) - min(d[1], 4 - d[1]) - 2 * d[2],
    )
)


def parts(x):
    hi = x.astype(np.float32).astype(ml_dtypes.bfloat16)
    lo = (x - hi.astype(np.float64)).astype(np.float32).astype(ml_dtypes.bfloat16)
    return hi, lo


def left_table(x):
    hi, lo = parts(x)
    return np.concatenate([hi, hi, lo], axis=1)


def right_table(x):
    hi, lo = parts(x)
    return np.concatenate([hi, hi, lo], axis=0)


def phases(rows, cols):
    angle = STEP * np.mod(np.outer(rows, cols), NG)
    return np.cos(angle), np.sin(angle)


def build_tables():
    grid = np.arange(NG)
    tables = {}
    kz = 2 * np.arange(KH)[None, :] + np.arange(2)[:, None]
    valid = (kz <= 64).reshape(-1).astype(np.float64)
    c, s = phases(grid, kz.reshape(-1) - 32)
    c, s = (c * valid).reshape(NG, 2, KH), (s * valid).reshape(NG, 2, KH)
    up = np.zeros((NG, 2, 2, 2, KH))
    up[:, 0, :, 0], up[:, 0, :, 1], up[:, 1, :, 0], up[:, 1, :, 1] = c, -s, s, c
    tables["z_up"] = left_table(up.reshape(2 * NG, 4 * KH))
    down = np.zeros((NG, 2, 2, 2, KH))
    down[:, 0, :, 0], down[:, 1, :, 0], down[:, 0, :, 1], down[:, 1, :, 1] = c, s, -s, c
    tables["z_down"] = left_table(down.reshape(2 * NG, 4 * KH).T)

    c, s = phases(np.arange(64) - 32, grid)
    hi, lo = parts(np.concatenate([c, s], axis=1))
    none = np.zeros_like(lo)
    tables["y_even"] = np.concatenate([hi, hi, lo, none])
    tables["y_odd"] = np.concatenate([hi, hi, none, lo])
    y_down = np.zeros((2, NG, 2, 2, 64))
    for j in range(2):
        y_down[j, :, 0, j], y_down[j, :, 1, j] = c.T, s.T
    tables["y_down"] = right_table(y_down.reshape(256, 256))

    wx = 4 * np.arange(NR)[None, :] + np.arange(4)[:, None] - 32
    c, s = phases(grid, wx.reshape(-1))
    x_up = np.zeros((2, NG, NX))
    x_up[:, :, : 8 * NR] = np.stack([np.concatenate([c, -s], axis=1), np.concatenate([s, c], axis=1)])
    for first, w in ((8 * NR, 32), (8 * NR + 2, 0)):
        c, s = phases(grid, np.array([w]))
        x_up[0, :, first], x_up[0, :, first + 1] = c[:, 0], -s[:, 0]
        x_up[1, :, first], x_up[1, :, first + 1] = s[:, 0], c[:, 0]
    tables["x_up"] = left_table(TO_GRID * x_up.reshape(2 * NG, NX))
    tables["x_down"] = left_table(TO_SPHERE * x_up.reshape(2 * NG, NX).T)

    c, s = phases(grid, np.arange(64))
    fwd = np.zeros((NG, 2, 64))
    fwd[:, 0], fwd[:, 1] = c, -s
    sign = np.where(grid % 2 == 0, 1.0, -1.0)
    fwd[:, 1, 0] = sign
    tables["py"] = right_table(fwd.reshape(NG, NG))
    inv = np.zeros((2, 64, NG))
    inv[0], inv[1] = 2.0 * c.T, -2.0 * s.T
    inv[0, 0], inv[1, 0] = 1.0, sign
    tables["piy"] = right_table(inv.reshape(NG, NG))
    c, s = phases(grid, grid)
    tables["px"] = left_table(np.concatenate([c, s], axis=1))
    tables["pix"] = left_table(np.concatenate([c, -s], axis=1))
    pairs = np.concatenate([grid[0::2], grid[1::2]])
    tables["pixp"] = left_table(np.concatenate([c[:, pairs], -s[:, pairs]], axis=1))
    order = (4 * np.arange(NP)[None, :] + np.arange(4)[:, None]).reshape(-1)
    tables["pz"] = left_table(np.concatenate([c[:, order], s[:, order]], axis=1))
    tables["piz"] = left_table(np.concatenate([c[order], -s[order]], axis=1))

    wk = np.where(grid < 64, grid, grid - NG)
    gauss = np.exp(-(wk**2) / (2.0 * WIDTH * WIDTH))
    g = np.cos(STEP * np.mod(np.outer(grid, grid), NG)) @ gauss
    circ = g[np.mod(grid[:, None] - grid[None, :], NG)]
    tables["circ"] = np.concatenate(parts(circ), axis=1)
    return tables


TABLES = build_tables()
NAMES = ("z_up", "y_even", "y_odd", "x_up", "py", "px", "circ", "pz", "piz", "pixp", "piy", "x_down", "y_down", "z_down", "pix")


def mm(a, b):
    return lax.dot_general(a, b, (((1,), (0,)), ((), ())), preferred_element_type=F32)


def mm_nt(a, b):
    return lax.dot_general(a, b, (((1,), (1,)), ((), ())), preferred_element_type=F32)


def split(x):
    hi = x.astype(BF16)
    return hi, (x - hi.astype(F32)).astype(BF16)


def stack_rows(x):
    hi, lo = split(x)
    return jnp.concatenate([hi, lo, hi], axis=0)


def stack_lanes(x):
    hi, lo = split(x)
    return jnp.concatenate([hi, lo, hi], axis=1)


def total(x):
    return jnp.sum(jnp.sum(x, axis=0, keepdims=True), axis=1, keepdims=True)


def iota(shape, axis):
    return lax.broadcasted_iota(jnp.int32, shape, axis)


def wrapped(x):
    return jnp.where(x < NG // 2, x, x - NG)


def turned(x):
    sgn = jnp.where(iota((1, 128), 1) < 64, 1.0, -1.0).astype(F32)
    blocks = [pltpu.roll(x[:, i : i + 128], 64, 1) * sgn for i in range(0, x.shape[1], 128)]
    return jnp.concatenate(blocks, axis=1)


def lanes_to_rows(x):
    return jnp.concatenate([x[:, i * 128 : (i + 1) * 128] for i in range(4)], axis=0)


def rows_to_lanes(x):
    return jnp.concatenate([x[i * 128 : (i + 1) * 128] for i in range(4)], axis=1)


def exponential_weights(first_energy, second_energy, spread):
    middle = 0.5 * (first_energy + second_energy)
    half_gap = 0.5 * (first_energy - second_energy)
    radius = jnp.sqrt(half_gap * half_gap + spread * spread)
    cosine = jnp.cos(TIME_STEP * radius)
    sine = jnp.sin(TIME_STEP * radius)
    along_first = sine * half_gap / radius
    along_second = sine * spread / radius
    phase_cos = jnp.cos(TIME_STEP * middle)
    phase_sin = jnp.sin(TIME_STEP * middle)
    weight_first = (
        phase_cos * cosine - phase_sin * along_first,
        -phase_cos * along_first - phase_sin * cosine,
    )
    weight_second = (-phase_sin * along_second, -phase_cos * along_second)
    return (weight_first, weight_second)


def kernel(coeffs_in, occ_in, cols_in, slots_in, atoms_in, *refs):
    t = dict(zip(NAMES, refs[: len(NAMES)]))
    held = dict(zip(NAMES, refs[-len(NAMES) - 1 : -1]))
    tsem = refs[-1]
    (new_out, dens_out, coeffs, occ, cols, slots, atoms, new, dens_val, sh, sht, cz, kin, tt, mt, ms, field, slv, cpad, apad, vloc, pot, wvec, sb1, rb1, xb, rsb, sbuf, tb, rb2,
     ub, rbv, dk, sb4, rb4, sb5, rb5, sbr, rbr, gz, ssem, rsem, isem, osem) = refs[len(NAMES) : -len(NAMES) - 1]
    me = lax.axis_index("pw")
    band = lax.axis_index("band")

    loads = {k: pltpu.make_async_copy(t[k], held[k], tsem.at[i]) for i, k in enumerate(NAMES)}
    inputs = (slots_in, slots), (coeffs_in, coeffs), (cols_in, cols), (occ_in, occ), (atoms_in, atoms)
    inputs = [pltpu.make_async_copy(a, b, isem.at[i]) for i, (a, b) in enumerate(inputs)]
    for copy in inputs:
        copy.start()

    def table(k):
        if k in loads:
            loads.pop(k).wait()
        return held[k][...]

    barrier = pltpu.get_barrier_semaphore()

    def greet_pw(i, carry):
        pl.semaphore_signal(barrier, inc=1, device_id={"pw": lax.rem(me + i, NP)}, device_id_type=MESH)
        return carry

    def greet_band(i, carry):
        pl.semaphore_signal(barrier, inc=1, device_id={"band": lax.rem(band + i, NB)}, device_id_type=MESH)
        return carry

    lax.fori_loop(1, NP, greet_pw, 0)
    lax.fori_loop(1, NB, greet_band, 0)
    for k in NAMES:
        loads[k].start()

    at_x, at_y, at_core = lax.div(me, 8), lax.rem(lax.div(me, 2), 4), lax.rem(me, 2)

    def peer(offset):
        x, y, core = offset
        return lax.rem(at_x + x, 4) * 8 + lax.rem(at_y + y, 4) * 2 + lax.rem(at_core + core, 2)

    due = {}
    gone = {}

    def send_pw(src, dst, k):
        due[k], gone[k] = dst, dst.at[pl.ds(0, NP - 1)]
        pltpu.make_async_copy(src.at[me], dst.at[me], rsem.at[k]).start()

        for offset in PEERS:
            to = peer(offset)
            pltpu.make_async_remote_copy(
                src.at[to], dst.at[me], ssem.at[k], rsem.at[k], device_id={"pw": to}, device_id_type=MESH
            ).start()

    def send_band(src, dst, whole, k):
        due[k], gone[k] = whole, whole.at[pl.ds(0, whole.shape[0] // NB * (NB - 1))]
        pltpu.make_async_copy(src(band), dst, rsem.at[k]).start()

        for i in FAR_FIRST:
            to = lax.rem(band + i, NB)
            pltpu.make_async_remote_copy(
                src(to), dst, ssem.at[k], rsem.at[k], device_id={"band": to}, device_id_type=MESH
            ).start()

    def arrive(k):
        ref = due.pop(k)
        pltpu.make_async_copy(ref, ref, rsem.at[k]).wait()

    def finish():
        for k, ref in gone.items():
            pltpu.make_async_copy(ref, ref, ssem.at[k]).wait()

    inputs[0].wait()
    for i in range(NPW_DEV // 128):
        slv[:, i * 128 : (i + 1) * 128] = slots[i : i + 1]
    slot = slv[...]
    stick = lax.shift_right_logical(slot, 7)
    zval = lax.bitwise_and(slot, 127)
    kzi = lax.bitwise_and(zval + 32, 127)
    khi = lax.shift_right_logical(kzi, 1)
    sh[...] = (iota((256, NPW_DEV), 0) == lax.bitwise_and(kzi, 1) * 128 + stick).astype(BF16)

    def scatter(re, im, late):
        hit = iota((KH, NPW_DEV), 0) == khi
        re_hi = re.astype(BF16).astype(F32)
        im_hi = im.astype(BF16).astype(F32)
        for k, pair in enumerate(((re_hi, im_hi), (re - re_hi, im - im_hi))):
            rows = jnp.concatenate([jnp.where(hit, x, 0.0) for x in pair], axis=0)
            cz[k * 2 * KH : (k + 1) * 2 * KH] = rows.astype(BF16)
        g = mm(cz[...], sht[...]) if late else mm_nt(cz[...], sh[...])
        g = g[: 2 * KH] + g[2 * KH :]
        g = jnp.concatenate([g[:, :128], g[:, 128:]], axis=0)
        return mm(table("z_up"), stack_rows(g)).reshape(NP, 8, 128)

    inputs[1].wait()
    sb1[0] = scatter(coeffs[0, 0:1], coeffs[1, 0:1], False)
    pl.semaphore_wait(barrier, NP - 1 + NB - 1)
    send_pw(sb1.at[0], rb1.at[0], A1)
    sb1[1] = scatter(coeffs[0, 1:2], coeffs[1, 1:2], False)
    send_pw(sb1.at[1], rb1.at[1], A1 + 1)

    inputs[2].wait()
    lane8 = iota((8, 128), 1)
    c = cols[...]
    xp = lax.bitwise_and(lax.shift_right_arithmetic(c, 7) + 32, 127)
    yp = lax.bitwise_and(c + 32, 127)
    far_x = xp == 64
    far_y = yp == 64
    regular = jnp.logical_and(xp < 64, yp < 64)
    r = jnp.where(regular, lax.shift_right_logical(xp, 2), -1)
    q = lax.bitwise_and(xp, 3) * 64 + yp
    for p in range(NQ):
        at = slice(p * 128, (p + 1) * 128)
        mt[:, at] = (iota((NR, 128), 0) == r[p : p + 1]).astype(F32)
        tt[:, at] = (iota((256, 128), 0) == q[p : p + 1]).astype(BF16)
        ms[0:1, at] = far_x[p : p + 1].astype(F32)
        ms[1:2, at] = far_y[p : p + 1].astype(F32)

    inputs[3].wait()
    inputs[4].wait()

    quarter = lax.bitwise_and(iota((1, 128), 1), 3)
    cos_b = jnp.where(quarter == 0, 1.0, jnp.where(quarter == 2, -1.0, 0.0))
    sin_b = jnp.where(quarter == 1, 1.0, jnp.where(quarter == 3, -1.0, 0.0))

    def to_field(rb):
        g = None
        ends = [jnp.zeros((8, 128), F32), jnp.zeros((8, 128), F32)]
        for p0 in range(0, NP, 4):
            d0, d1, d2, d3 = (rb[p0 + i] for i in range(4))
            d1, d2, d3 = pltpu.roll(d1, 96, 1), pltpu.roll(d2, 64, 1), pltpu.roll(d3, 32, 1)
            packed = (
                jnp.where(lane8 < 96, d0, d1),
                jnp.where(lane8 < 64, d1, d2),
                jnp.where(lane8 < 32, d2, d3),
            )
            block = []
            q0 = p0 // 4 * 3
            for p, d in enumerate(packed, q0):
                m = mt[:, p * 128 : (p + 1) * 128]
                ends = [x + d * ms[i : i + 1, p * 128 : (p + 1) * 128] for i, x in enumerate(ends)]
                hi = d.astype(BF16).astype(F32)
                rows = [jnp.broadcast_to(v[i : i + 1], (NR, 128)) * m for v in (hi, d - hi) for i in range(8)]
                block.append(jnp.concatenate(rows, axis=0).astype(BF16))
            y = mm_nt(jnp.concatenate(block, axis=1), tt[:, q0 * 128 : (q0 + 3) * 128])
            g = y if g is None else g + y
        g = g[: 8 * NR] + g[8 * NR :]
        hi = g.astype(BF16).astype(F32)
        lo = g - hi
        left = iota((1, 128), 1) < 64
        re, im = [], []
        for j in range(4):
            at = slice(j // 2 * 128, j // 2 * 128 + 128)
            h, l = hi[:, at], pltpu.roll(lo[:, at], 64, 1)
            both = jnp.where(left, h, l) if j % 2 == 0 else jnp.where(left, l, h)
            f = jnp.concatenate([both, h], axis=1).astype(BF16)
            f = mm(f, table("y_even" if j % 2 == 0 else "y_odd"))
            row_re, row_im = [], []
            for z in range(4):
                a = f[(2 * z) * NR : (2 * z + 1) * NR]
                b = f[(2 * z + 1) * NR : (2 * z + 2) * NR]
                row_re.append(a[:, :128] - b[:, 128:])
                row_im.append(a[:, 128:] + b[:, :128])
            re.append(jnp.concatenate(row_re, axis=1))
            im.append(jnp.concatenate(row_im, axis=1))
        rows = re + im
        ex, ey = (jnp.sum(x, axis=1, keepdims=True) for x in ends)
        extra = []
        for z in range(4):
            k = 2 * z
            yr, yi = ey[k : k + 1], ey[k + 1 : k + 2]
            x = jnp.broadcast_to(ex[k : k + 2], (2, 128))
            y = [yr * cos_b - yi * sin_b, yr * sin_b + yi * cos_b]
            extra.append(jnp.concatenate([x] + y + [jnp.zeros((12, 128), F32)], axis=0))
        rows.append(jnp.concatenate(extra, axis=1))
        return mm(table("x_up"), stack_rows(jnp.concatenate(rows, axis=0)))

    dens = None
    for n in range(2):
        arrive(A1 + n)
        f = to_field(rb1.at[n])
        field[n] = f
        term = (f[:128] * f[:128] + f[128:] * f[128:]) * (occ[n] * (1.0 / 16.0))
        dens = term if dens is None else dens + term

    def plane_x(x, name):
        flipped = jnp.concatenate([turned(x[:, z * 128 : (z + 1) * 128]) for z in range(4)], axis=1)
        return mm(table(name), stack_rows(jnp.concatenate([x, flipped], axis=0)))

    def plane_inverse(x, name):
        y = plane_x(x, name)
        return rows_to_lanes(mm(stack_lanes(lanes_to_rows(y)), table("piy")))

    means = []
    for z in range(4):
        means.append(total(dens[:, z * 128 : (z + 1) * 128]) * (1.0 / (NG * NG)))
    mean = jnp.concatenate([jnp.broadcast_to(m, (1, 128)) for m in means], axis=1)
    dens = dens - mean
    xb[...] = plane_x(rows_to_lanes(mm(stack_lanes(lanes_to_rows(dens)), table("py"))), "px")
    head = jnp.where(lax.bitwise_and(iota((8, 512), 1), 127) == 0, mean * float(NG * NG), 0.0)
    xb[0:8] = xb[0:8] + jnp.where(iota((8, 512), 0) == 0, head, 0.0)
    send_band(lambda to: xb.at[pl.ds(pl.multiple_of(16 * to, 16), 16)], rsb.at[band], rsb, RS)

    c0, c1, c2 = (cols[pl.ds(i, 8, stride=3), :] for i in range(3))
    blocks = (
        c0,
        jnp.where(lane8 < 32, pltpu.roll(c0, 32, 1), pltpu.roll(c1, 32, 1)),
        jnp.where(lane8 < 64, pltpu.roll(c1, 64, 1), pltpu.roll(c2, 64, 1)),
        pltpu.roll(c2, 96, 1),
    )
    for i, block in enumerate(blocks):
        cpad[pl.ds(i, 8, stride=4), :] = jnp.where(lane8 < ST, block, -1)
    own = cpad[pl.ds(me, 1), :]
    wx = wrapped(lax.bitwise_and(lax.shift_right_arithmetic(own, 7), 127))
    wy = wrapped(lax.bitwise_and(own, 127))
    reach = wx * wx + wy * wy
    coarse = lax.shift_right_logical(reach, 5).astype(F32)
    fine = lax.bitwise_and(reach, 31).astype(F32)
    both = jnp.concatenate([jnp.broadcast_to(coarse, (8, 128)), jnp.broadcast_to(fine, (8, 128))], axis=0)
    picked = mm(jnp.concatenate([both, both], axis=1).astype(BF16), sh[...])
    wz = wrapped(zval)
    kin[...] = (123.4 / (NG * NG)) * (32.0 * picked[0:1] + picked[8:9] + (wz * wz).astype(F32))

    apad[...] = jnp.full((3, 1024), -1, jnp.int32)
    apad[:, : atoms.shape[1]] = atoms[...]

    def spots(row):
        hot = (iota((128, 1024), 0) == apad[row : row + 1]).astype(BF16)
        return mm(table("circ"), jnp.concatenate([hot, hot], axis=0))

    gz[...] = spots(2)
    gy_hi, gy_lo = split(spots(1))
    gx = spots(0) * FORM
    for z in range(4):
        gl = gx * gz[pl.ds(4 * me + z, 1), :]
        g_hi, g_lo = split(gl)
        vloc[:, z * 128 : (z + 1) * 128] = mm_nt(g_hi, gy_hi) + mm_nt(g_lo, gy_hi) + mm_nt(g_hi, gy_lo)

    lane = iota((128, 256), 1)
    wkz = wrapped(iota((128, 256), 0))
    kx = 16 * band + 2 * lax.div(me, 4) + lax.shift_right_logical(lane, 7)
    lane = lax.bitwise_and(lane, 127)
    wkx = wrapped(kx)
    ky = lax.bitwise_and(lane, 63)
    q = wkz * wkz + wkx * wkx + ky * ky
    corner = jnp.logical_and(q == 0, lane == 64)
    q = jnp.where(corner, 4096, q).astype(F32)
    factor = jnp.where(q > 0.0, (HARTREE / NG**3) / jnp.maximum(q, 1.0), 0.0)

    def transpose(i, carry):
        at = pl.ds(pl.multiple_of(i * 512, 512), 512)
        sht[at, :] = sh[:, at].T
        return carry

    lax.fori_loop(0, NPW_DEV // 512, transpose, 0)
    arrive(RS)
    s = rsb[0]
    for i in range(1, NB):
        s = s + rsb[i]
    sbuf[...] = s
    for i in range(8):
        for z in range(4):
            tb[i, 2 * z : 2 * z + 2, :] = s[2 * i : 2 * i + 2, z * 128 : (z + 1) * 128]
    mine = lax.div(me, 4)
    slot_me = pl.ds(pl.multiple_of(8 * me, 8), 8)
    pltpu.make_async_copy(tb.at[mine], rb2.at[slot_me], rsem.at[A2]).start()

    for offset in PEERS:
        to = peer(offset)
        pltpu.make_async_remote_copy(
            tb.at[lax.div(to, 4)], rb2.at[slot_me], ssem.at[A2], rsem.at[A2], device_id={"pw": to}, device_id_type=MESH
        ).start()
    due[A2], gone[A2] = rb2, rb2.at[pl.ds(0, 8 * (NP - 1))]

    arrive(A2)
    x = [
        jnp.concatenate([rb2[pl.ds(2 * z + k, NP, stride=8), :] for z in range(4)], axis=0) for k in range(2)
    ]
    x = jnp.concatenate(x, axis=1)
    flat = jnp.logical_and(lane == 0, kx == 0)
    x = x - jnp.where(flat, jnp.sum(jnp.where(flat, x, 0.0), axis=0, keepdims=True) * (1.0 / NG), 0.0)
    x = mm(table("pz"), stack_rows(jnp.concatenate([x, turned(x)], axis=0))) * factor
    x = mm(table("piz"), stack_rows(jnp.concatenate([x, turned(x)], axis=0)))
    for z in range(4):
        for k in range(2):
            ub[pl.ds(2 * z + k, NP, stride=8), :] = x[z * NP : (z + 1) * NP, k * 128 : (k + 1) * 128]
    low = lax.rem(me, 4)
    turn = band * 8 + mine
    place = pl.ds(pl.multiple_of(8 * turn, 8), 8)
    pltpu.make_async_copy(ub.at[slot_me], rbv.at[place], rsem.at[A3]).start()

    for away, x, half in TARGETS:
        spot = peer((x, 2 * half, 0))
        pltpu.make_async_remote_copy(
            ub.at[pl.ds(pl.multiple_of(8 * spot, 8), 8)],
            rbv.at[place],
            ssem.at[A3],
            rsem.at[A3],
            device_id={"band": lax.rem(band + away, NB), "pw": spot},
            device_id_type=MESH,
        ).start()
    due[A3], gone[A3] = rbv, rbv.at[pl.ds(0, 8 * 63)]
    arrive(A3)
    vk = [
        jnp.concatenate([rbv[pl.ds(2 * z + k, 64, stride=8), :] for k in range(2)], axis=0) for z in range(4)
    ]
    pot[...] = plane_inverse(jnp.concatenate(vk, axis=1), "pixp") + vloc[...]

    lane1 = iota((8, 128), 1)
    weight = NPW / NG**3
    for n in range(2):
        f = field[n]
        v = pot[...]
        u = jnp.concatenate([v * f[:128], v * f[128:]], axis=0)
        nsq_part = total(coeffs[0, n : n + 1] * coeffs[0, n : n + 1] + coeffs[1, n : n + 1] * coeffs[1, n : n + 1])
        cross_part = weight * total(u[:128] * f[:128] + u[128:] * f[128:]) + total(
            kin[...]
            * (coeffs[0, n : n + 1] * coeffs[0, n : n + 1] + coeffs[1, n : n + 1] * coeffs[1, n : n + 1])
        )
        x = mm(table("x_down"), stack_rows(u))
        tiles = []
        for t in range(2):
            rows = [
                jnp.concatenate(
                    [x[(c * 4 + j) * NR : (c * 4 + j + 1) * NR, z * 128 : (z + 1) * 128] for j in (2 * t, 2 * t + 1)],
                    axis=1,
                )
                for z in range(4)
                for c in range(2)
            ]
            o = mm(stack_lanes(jnp.concatenate(rows, axis=0)), table("y_down"))
            rows = []
            for z in range(4):
                a = o[(2 * z) * NR : (2 * z + 1) * NR]
                b = o[(2 * z + 1) * NR : (2 * z + 2) * NR]
                rows.append(a[:, :128] + b[:, 128:])
                rows.append(b[:, :128] - a[:, 128:])
            tiles.append(jnp.concatenate(rows, axis=0))
        hi, lo = split(jnp.concatenate(tiles, axis=1))
        edge = x[8 * NR :]
        ex, ey = [], []
        for z in range(4):
            a, b, c, d = (edge[i : i + 1, z * 128 : (z + 1) * 128] for i in range(4))
            ex += [a, b]
            ey += [c * cos_b + d * sin_b, d * cos_b - c * sin_b]
        ex, ey = (jnp.sum(jnp.concatenate(v, axis=0), axis=1, keepdims=True) for v in (ex, ey))
        extra = jnp.where(lane1 == 96, nsq_part, 0.0) + jnp.where(lane1 == 97, cross_part, 0.0)

        y = mm(jnp.concatenate([hi, lo], axis=0), tt[...])
        y = y[: 8 * NR] + y[8 * NR :]
        m = mt[...]
        y = jnp.concatenate(
            [jnp.sum(y[k * NR : (k + 1) * NR] * m, axis=0, keepdims=True) for k in range(8)], axis=0
        )
        y = y + ex * ms[0:1] + ey * ms[1:2]
        for g in range(NP // 4):
            t0, t1, t2 = (y[:, (3 * g + i) * 128 : (3 * g + i + 1) * 128] for i in range(3))
            blocks = (
                t0,
                jnp.where(lane8 < 32, pltpu.roll(t0, 32, 1), pltpu.roll(t1, 32, 1)),
                jnp.where(lane8 < 64, pltpu.roll(t1, 64, 1), pltpu.roll(t2, 64, 1)),
                pltpu.roll(t2, 96, 1),
            )
            for i, block in enumerate(blocks):
                sb4[n, 4 * g + i] = jnp.where(lane8 < ST, block, extra)
        send_pw(sb4.at[n], rb4.at[n], A4 + n)

    at_band = pl.ds(pl.multiple_of(16 * band, 16), 16)
    send_band(lambda to: sbuf, dk.at[at_band], dk, AGD)

    states = []
    for n in range(2):
        arrive(A4 + n)
        r = rb4[n]
        ends = jnp.sum(r, axis=0)[0:1]
        nsq = jnp.sum(jnp.where(iota((1, 128), 1) == 96, ends, 0.0), axis=1, keepdims=True) + EPSILON
        cross = jnp.sum(jnp.where(iota((1, 128), 1) == 97, ends, 0.0), axis=1, keepdims=True)
        alpha0 = cross / nsq
        g = mm(table("z_down"), stack_rows(r.reshape(256, 128)))
        hi, lo = split(jnp.concatenate([g[: 2 * KH], g[2 * KH :]], axis=1))
        y = mm(jnp.concatenate([hi, lo], axis=0), sh[...])
        y = y[: 2 * KH] + y[2 * KH :]
        pick = iota((KH, NPW_DEV), 0) == khi
        for c in range(2):
            part = jnp.sum(jnp.where(pick, y[c * KH : (c + 1) * KH], 0.0), axis=0, keepdims=True)
            wvec[n, c : c + 1] = part + (kin[...] - alpha0) * coeffs[c, n : n + 1]
        w_re = wvec[n, 0:1]
        w_im = wvec[n, 1:2]
        sb5[n] = scatter(w_re, w_im, True)
        send_pw(sb5.at[n], rb5.at[n], A5 + n)
        wsq = w_re * w_re + w_im * w_im
        states.append((nsq, alpha0, total(wsq), total(wsq * kin[...])))

    out = jnp.zeros((8, 128), F32)
    for n in range(2):
        arrive(A5 + n)
        f = to_field(rb5.at[n])
        energy = weight * total(pot[...] * (f[:128] * f[:128] + f[128:] * f[128:])) + states[n][3]
        out = out + jnp.where(lane1 == 2 * n, states[n][2], 0.0) + jnp.where(lane1 == 2 * n + 1, energy, 0.0)
    sbr[...] = out[0:1]
    pltpu.make_async_copy(sbr, rbr.at[me], rsem.at[AR]).start()

    for offset in PEERS:
        to = peer(offset)
        pltpu.make_async_remote_copy(
            sbr, rbr.at[me], ssem.at[AR], rsem.at[AR], device_id={"pw": to}, device_id_type=MESH
        ).start()
    due[AR], gone[AR] = rbr, rbr.at[pl.ds(0, NP - 1)]
    arrive(AGD)
    d = plane_inverse(dk[...], "pix") * (1.0 / (NG * NG))
    for z in range(4):
        dens_val[z] = d[:, z * 128 : (z + 1) * 128]
    dens_copy = pltpu.make_async_copy(dens_val, dens_out, osem.at[0])
    dens_copy.start()
    arrive(AR)
    ends = jnp.sum(rbr[...], axis=0)
    for n in range(2):
        nsq, alpha0 = states[n][0], states[n][1]
        ww = jnp.sum(jnp.where(iota((1, 128), 1) == 2 * n, ends, 0.0), axis=1, keepdims=True)
        ew = jnp.sum(jnp.where(iota((1, 128), 1) == 2 * n + 1, ends, 0.0), axis=1, keepdims=True)
        spread_sq = ww / nsq + EPSILON
        spread = jnp.sqrt(spread_sq)
        alpha1 = ew / (nsq * spread_sq)
        first, second = exponential_weights(alpha0, alpha1, spread)
        sec_re = second[0] / spread
        sec_im = second[1] / spread
        c_re, c_im = coeffs[0, n : n + 1], coeffs[1, n : n + 1]
        w_re, w_im = wvec[n, 0:1], wvec[n, 1:2]
        new[0, n : n + 1] = first[0] * c_re - first[1] * c_im + (sec_re * w_re - sec_im * w_im)
        new[1, n : n + 1] = first[0] * c_im + first[1] * c_re + (sec_re * w_im + sec_im * w_re)

    new_copy = pltpu.make_async_copy(new, new_out, osem.at[1])
    new_copy.start()
    finish()
    dens_copy.wait()
    new_copy.wait()


def copies(new_in, dens_in, new_out, dens_out):
    new_out[...] = new_in[...]
    dens_out[...] = dens_in[...]


def local(coeffs, occupation, stick_columns, sphere_slots, atom_sites):
    cols = stick_columns.reshape(NP * ST // 128, 128)
    slots = sphere_slots.reshape(NPW_DEV // 128, 128)
    hbm = pl.BlockSpec(memory_space=pl.ANY)
    vm = pl.BlockSpec(memory_space=pltpu.VMEM)
    tables = [jnp.asarray(TABLES[k]) for k in NAMES]
    V = pltpu.VMEM
    results = (
        jax.ShapeDtypeStruct((2, 2, NPW_DEV), F32),
        jax.ShapeDtypeStruct((4, NG, NG), F32),
    )
    step = pl.pallas_call(
        kernel,
        out_shape=results,
        in_specs=[hbm] * (5 + len(NAMES)),
        out_specs=(hbm, hbm),
        scratch_shapes=[
            V((2, 2, NPW_DEV), F32),
            pltpu.SMEM((2,), F32),
            V((NP * ST // 128, 128), jnp.int32),
            V((NPW_DEV // 128, 128), jnp.int32),
            V(atom_sites.shape, jnp.int32),
            V((2, 2, NPW_DEV), F32),
            V((4, NG, NG), F32),
            V((256, NPW_DEV), BF16),
            V((NPW_DEV, 256), BF16),
            V((4 * KH, NPW_DEV), BF16),
            V((1, NPW_DEV), F32),
            V((256, NQ * 128), BF16),
            V((NR, NQ * 128), F32),
            V((2, NQ * 128), F32),
            V((2, 256, 512), F32),
            V((1, NPW_DEV), jnp.int32),
            V((NP, 128), jnp.int32),
            V((3, 1024), jnp.int32),
            V((128, 512), F32),
            V((128, 512), F32),
            V((2, 2, NPW_DEV), F32),
            V((2, NP, 8, 128), F32),
            V((2, NP, 8, 128), F32),
            V((128, 512), F32),
            V((NB, 16, 512), F32),
            V((16, 512), F32),
            V((8, 8, 128), F32),
            V((8 * NP, 128), F32),
            V((8 * NP, 128), F32),
            V((512, 128), F32),
            V((128, 512), F32),
            V((2, NP, 8, 128), F32),
            V((2, NP, 8, 128), F32),
            V((2, NP, 8, 128), F32),
            V((2, NP, 8, 128), F32),
            V((1, 128), F32),
            V((NP, 1, 128), F32),
            V((128, 1024), F32),
            pltpu.SemaphoreType.DMA((N_SEM,)),
            pltpu.SemaphoreType.DMA((N_SEM,)),
            pltpu.SemaphoreType.DMA((5,)),
            pltpu.SemaphoreType.DMA((2,)),
        ]
        + [V(TABLES[k].shape, BF16) for k in NAMES]
        + [pltpu.SemaphoreType.DMA((len(NAMES),))],
        compiler_params=pltpu.CompilerParams(
            collective_id=0, has_side_effects=True, vmem_limit_bytes=60 * 1024 * 1024
        ),
        name="step",
    )(coeffs, occupation, cols, slots, atom_sites, *tables)
    return pl.pallas_call(
        copies,
        out_shape=results,
        in_specs=[vm, vm],
        out_specs=(vm, vm),
        name="results",
    )(*step)


def solution(mesh):
    in_specs = (P(None, "band", "pw"), P("band"), P(), P("pw"), P())
    out_specs = (P(None, "band", "pw"), P("pw", None, None))
    return jax.shard_map(local, mesh=mesh, in_specs=in_specs, out_specs=out_specs, check_vma=False)
```

```python
import functools
import math

import jax
import jax.numpy as jnp
import numpy as np
import ml_dtypes
from jax import lax
from jax.experimental import pallas as pl
from jax.experimental.pallas import tpu as pltpu
from jax.sharding import PartitionSpec as P

MESH = pl.DeviceIdType.MESH
F32 = jnp.float32
BF16 = jnp.bfloat16

NG = 128
NP = 32
NB = 8
NPW_DEV = 3584
NPW = NPW_DEV * NP
ST = 96
KH = 40
NR = 16
NQ = NP * ST // 128
NX = 8 * NR + 16
TIME_STEP = 0.2
EPSILON = 1e-06
STEP = 2.0 * math.pi / NG
WIDTH = NG / 20.0
FORM = -2.0 / ((2.0 * math.pi) ** 1.5 * WIDTH**3)
TO_GRID = 1.0 / math.sqrt(NPW)
TO_SPHERE = math.sqrt(NPW) / NG**3
HARTREE = 0.1 * NG * NG

A1, RS, A2, A3, AGV, AGD, A4, A5, AR = 0, 2, 3, 4, 5, 6, 7, 9, 11
N_SEM = 12
PEERS = tuple(sorted(((x, y, c) for x in range(4) for y in range(4) for c in (0, 1) if x or y or c), key=lambda d: (-min(d[0], 4 - d[0]) - min(d[1], 4 - d[1]), (d[0] + 3 * d[1]) % 4, d[2])))
FAR_FIRST = (4, 3, 5, 2, 6, 1, 7)
TARGETS = tuple(
    sorted(
        ((b, x, h) for x in (2, 1, 3, 0) for h in (1, 0) for b in FAR_FIRST + (0,) if b or x or h),
        key=lambda d: -min(d[0], 8 - d[0]) - min(d[1], 4 - d[1]) - 2 * d[2],
    )
)


def parts(x):
    hi = x.astype(np.float32).astype(ml_dtypes.bfloat16)
    lo = (x - hi.astype(np.float64)).astype(np.float32).astype(ml_dtypes.bfloat16)
    return hi, lo


def left_table(x):
    hi, lo = parts(x)
    return np.concatenate([hi, hi, lo], axis=1)


def right_table(x):
    hi, lo = parts(x)
    return np.concatenate([hi, hi, lo], axis=0)


def phases(rows, cols):
    angle = STEP * np.mod(np.outer(rows, cols), NG)
    return np.cos(angle), np.sin(angle)


def build_tables():
    grid = np.arange(NG)
    tables = {}
    kz = 2 * np.arange(KH)[None, :] + np.arange(2)[:, None]
    valid = (kz <= 64).reshape(-1).astype(np.float64)
    c, s = phases(grid, kz.reshape(-1) - 32)
    c, s = (c * valid).reshape(NG, 2, KH), (s * valid).reshape(NG, 2, KH)
    up = np.zeros((NG, 2, 2, 2, KH))
    up[:, 0, :, 0], up[:, 0, :, 1], up[:, 1, :, 0], up[:, 1, :, 1] = c, -s, s, c
    tables["z_up"] = left_table(up.reshape(2 * NG, 4 * KH))
    down = np.zeros((NG, 2, 2, 2, KH))
    down[:, 0, :, 0], down[:, 1, :, 0], down[:, 0, :, 1], down[:, 1, :, 1] = c, s, -s, c
    tables["z_down"] = left_table(down.reshape(2 * NG, 4 * KH).T)

    c, s = phases(np.arange(64) - 32, grid)
    hi, lo = parts(np.concatenate([c, s], axis=1))
    none = np.zeros_like(lo)
    tables["y_even"] = np.concatenate([hi, hi, lo, none])
    tables["y_odd"] = np.concatenate([hi, hi, none, lo])
    y_down = np.zeros((2, NG, 2, 2, 64))
    for j in range(2):
        y_down[j, :, 0, j], y_down[j, :, 1, j] = c.T, s.T
    tables["y_down"] = right_table(y_down.reshape(256, 256))

    wx = 4 * np.arange(NR)[None, :] + np.arange(4)[:, None] - 32
    c, s = phases(grid, wx.reshape(-1))
    x_up = np.zeros((2, NG, NX))
    x_up[:, :, : 8 * NR] = np.stack([np.concatenate([c, -s], axis=1), np.concatenate([s, c], axis=1)])
    for first, w in ((8 * NR, 32), (8 * NR + 2, 0)):
        c, s = phases(grid, np.array([w]))
        x_up[0, :, first], x_up[0, :, first + 1] = c[:, 0], -s[:, 0]
        x_up[1, :, first], x_up[1, :, first + 1] = s[:, 0], c[:, 0]
    tables["x_up"] = left_table(TO_GRID * x_up.reshape(2 * NG, NX))
    tables["x_down"] = left_table(TO_SPHERE * x_up.reshape(2 * NG, NX).T)

    c, s = phases(grid, np.arange(64))
    fwd = np.zeros((NG, 2, 64))
    fwd[:, 0], fwd[:, 1] = c, -s
    sign = np.where(grid % 2 == 0, 1.0, -1.0)
    fwd[:, 1, 0] = sign
    tables["py"] = right_table(fwd.reshape(NG, NG))
    inv = np.zeros((2, 64, NG))
    inv[0], inv[1] = 2.0 * c.T, -2.0 * s.T
    inv[0, 0], inv[1, 0] = 1.0, sign
    tables["piy"] = right_table(inv.reshape(NG, NG))
    c, s = phases(grid, grid)
    tables["px"] = left_table(np.concatenate([c, s], axis=1))
    tables["pix"] = left_table(np.concatenate([c, -s], axis=1))
    pairs = np.concatenate([grid[0::2], grid[1::2]])
    tables["pixp"] = left_table(np.concatenate([c[:, pairs], -s[:, pairs]], axis=1))
    order = (4 * np.arange(NP)[None, :] + np.arange(4)[:, None]).reshape(-1)
    tables["pz"] = left_table(np.concatenate([c[:, order], s[:, order]], axis=1))
    tables["piz"] = left_table(np.concatenate([c[order], -s[order]], axis=1))

    wk = np.where(grid < 64, grid, grid - NG)
    gauss = np.exp(-(wk**2) / (2.0 * WIDTH * WIDTH))
    g = np.cos(STEP * np.mod(np.outer(grid, grid), NG)) @ gauss
    circ = g[np.mod(grid[:, None] - grid[None, :], NG)]
    tables["circ"] = np.concatenate(parts(circ), axis=1)
    return tables


TABLES = build_tables()
NAMES = ("z_up", "y_even", "y_odd", "x_up", "py", "px", "circ", "pz", "piz", "pixp", "piy", "x_down", "y_down", "z_down", "pix")


def mm(a, b):
    return lax.dot_general(a, b, (((1,), (0,)), ((), ())), preferred_element_type=F32)


def mm_nt(a, b):
    return lax.dot_general(a, b, (((1,), (1,)), ((), ())), preferred_element_type=F32)


def split(x):
    hi = x.astype(BF16)
    return hi, (x - hi.astype(F32)).astype(BF16)


def stack_rows(x):
    hi, lo = split(x)
    return jnp.concatenate([hi, lo, hi], axis=0)


def stack_lanes(x):
    hi, lo = split(x)
    return jnp.concatenate([hi, lo, hi], axis=1)


def total(x):
    return jnp.sum(jnp.sum(x, axis=0, keepdims=True), axis=1, keepdims=True)


def iota(shape, axis):
    return lax.broadcasted_iota(jnp.int32, shape, axis)


def wrapped(x):
    return jnp.where(x < NG // 2, x, x - NG)


def turned(x):
    sgn = jnp.where(iota((1, 128), 1) < 64, 1.0, -1.0).astype(F32)
    blocks = [pltpu.roll(x[:, i : i + 128], 64, 1) * sgn for i in range(0, x.shape[1], 128)]
    return jnp.concatenate(blocks, axis=1)


def lanes_to_rows(x):
    return jnp.concatenate([x[:, i * 128 : (i + 1) * 128] for i in range(4)], axis=0)


def rows_to_lanes(x):
    return jnp.concatenate([x[i * 128 : (i + 1) * 128] for i in range(4)], axis=1)


def exponential_weights(first_energy, second_energy, spread):
    middle = 0.5 * (first_energy + second_energy)
    half_gap = 0.5 * (first_energy - second_energy)
    radius = jnp.sqrt(half_gap * half_gap + spread * spread)
    cosine = jnp.cos(TIME_STEP * radius)
    sine = jnp.sin(TIME_STEP * radius)
    along_first = sine * half_gap / radius
    along_second = sine * spread / radius
    phase_cos = jnp.cos(TIME_STEP * middle)
    phase_sin = jnp.sin(TIME_STEP * middle)
    weight_first = (
        phase_cos * cosine - phase_sin * along_first,
        -phase_cos * along_first - phase_sin * cosine,
    )
    weight_second = (-phase_sin * along_second, -phase_cos * along_second)
    return (weight_first, weight_second)


def kernel(coeffs_in, occ_in, cols_in, slots_in, atoms_in, *refs):
    t = dict(zip(NAMES, refs[: len(NAMES)]))
    held = dict(zip(NAMES, refs[-len(NAMES) - 1 : -1]))
    tsem = refs[-1]
    (new_out, dens_out, coeffs, occ, cols, slots, atoms, new, dens_val, sh, sht, cz, kin, tt, mt, ms, field, slv, cpad, apad, vloc, pot, wvec, sb1, rb1, xb, rsb, sbuf, tb, rb2,
     ub, rbv, dk, sb4, rb4, sb5, rb5, sbr, rbr, gz, ssem, rsem, isem, osem) = refs[len(NAMES) : -len(NAMES) - 1]
    me = lax.axis_index("pw")
    band = lax.axis_index("band")

    loads = {k: pltpu.make_async_copy(t[k], held[k], tsem.at[i]) for i, k in enumerate(NAMES)}
    inputs = (slots_in, slots), (coeffs_in, coeffs), (cols_in, cols), (occ_in, occ), (atoms_in, atoms)
    inputs = [pltpu.make_async_copy(a, b, isem.at[i]) for i, (a, b) in enumerate(inputs)]
    for copy in inputs:
        copy.start()

    def table(k):
        if k in loads:
            loads.pop(k).wait()
        return held[k][...]

    barrier = pltpu.get_barrier_semaphore()

    at_x, at_y, at_core = lax.div(me, 8), lax.rem(lax.div(me, 2), 4), lax.rem(me, 2)

    def peer(offset):
        x, y, core = offset
        return lax.rem(at_x + x, 4) * 8 + lax.rem(at_y + y, 4) * 2 + lax.rem(at_core + core, 2)

    for offset in PEERS:
        pl.semaphore_signal(barrier, inc=1, device_id={"pw": peer(offset)}, device_id_type=MESH)
    for i in FAR_FIRST:
        pl.semaphore_signal(barrier, inc=1, device_id={"band": lax.rem(band + i, NB)}, device_id_type=MESH)
    for k in NAMES:
        loads[k].start()

    due = {}
    gone = {}

    def send_pw(src, dst, k):
        due[k], gone[k] = dst, dst.at[pl.ds(0, NP - 1)]
        pltpu.make_async_copy(src.at[me], dst.at[me], rsem.at[k]).start()

        for offset in PEERS:
            to = peer(offset)
            pltpu.make_async_remote_copy(
                src.at[to], dst.at[me], ssem.at[k], rsem.at[k], device_id={"pw": to}, device_id_type=MESH
            ).start()

    def send_band(src, dst, whole, k):
        due[k], gone[k] = whole, whole.at[pl.ds(0, whole.shape[0] // NB * (NB - 1))]
        pltpu.make_async_copy(src(band), dst, rsem.at[k]).start()

        for i in FAR_FIRST:
            to = lax.rem(band + i, NB)
            pltpu.make_async_remote_copy(
                src(to), dst, ssem.at[k], rsem.at[k], device_id={"band": to}, device_id_type=MESH
            ).start()

    def arrive(k):
        ref = due.pop(k)
        pltpu.make_async_copy(ref, ref, rsem.at[k]).wait()

    def finish():
        for k, ref in gone.items():
            pltpu.make_async_copy(ref, ref, ssem.at[k]).wait()

    inputs[0].wait()
    for i in range(NPW_DEV // 128):
        slv[:, i * 128 : (i + 1) * 128] = slots[i : i + 1]
    slot = slv[...]
    stick = lax.shift_right_logical(slot, 7)
    zval = lax.bitwise_and(slot, 127)
    kzi = lax.bitwise_and(zval + 32, 127)
    khi = lax.shift_right_logical(kzi, 1)
    sh[...] = (iota((256, NPW_DEV), 0) == lax.bitwise_and(kzi, 1) * 128 + stick).astype(BF16)

    def scatter(re, im, late):
        hit = iota((KH, NPW_DEV), 0) == khi
        re_hi = re.astype(BF16).astype(F32)
        im_hi = im.astype(BF16).astype(F32)
        for k, pair in enumerate(((re_hi, im_hi), (re - re_hi, im - im_hi))):
            rows = jnp.concatenate([jnp.where(hit, x, 0.0) for x in pair], axis=0)
            cz[k * 2 * KH : (k + 1) * 2 * KH] = rows.astype(BF16)
        g = mm(cz[...], sht[...]) if late else mm_nt(cz[...], sh[...])
        g = g[: 2 * KH] + g[2 * KH :]
        g = jnp.concatenate([g[:, :128], g[:, 128:]], axis=0)
        return mm(table("z_up"), stack_rows(g)).reshape(NP, 8, 128)

    inputs[1].wait()
    sb1[0] = scatter(coeffs[0, 0:1], coeffs[1, 0:1], False)
    pl.semaphore_wait(barrier, NP - 1 + NB - 1)
    send_pw(sb1.at[0], rb1.at[0], A1)
    sb1[1] = scatter(coeffs[0, 1:2], coeffs[1, 1:2], False)
    send_pw(sb1.at[1], rb1.at[1], A1 + 1)

    inputs[2].wait()
    lane8 = iota((8, 128), 1)
    c = cols[...]
    xp = lax.bitwise_and(lax.shift_right_arithmetic(c, 7) + 32, 127)
    yp = lax.bitwise_and(c + 32, 127)
    far_x = xp == 64
    far_y = yp == 64
    regular = jnp.logical_and(xp < 64, yp < 64)
    r = jnp.where(regular, lax.shift_right_logical(xp, 2), -1)
    q = lax.bitwise_and(xp, 3) * 64 + yp
    for p in range(NQ):
        at = slice(p * 128, (p + 1) * 128)
        mt[:, at] = (iota((NR, 128), 0) == r[p : p + 1]).astype(F32)
        tt[:, at] = (iota((256, 128), 0) == q[p : p + 1]).astype(BF16)
        ms[0:1, at] = far_x[p : p + 1].astype(F32)
        ms[1:2, at] = far_y[p : p + 1].astype(F32)

    inputs[3].wait()
    inputs[4].wait()

    quarter = lax.bitwise_and(iota((1, 128), 1), 3)
    cos_b = jnp.where(quarter == 0, 1.0, jnp.where(quarter == 2, -1.0, 0.0))
    sin_b = jnp.where(quarter == 1, 1.0, jnp.where(quarter == 3, -1.0, 0.0))

    def to_field(rb):
        g = None
        ends = [jnp.zeros((8, 128), F32), jnp.zeros((8, 128), F32)]
        for p0 in range(0, NP, 4):
            d0, d1, d2, d3 = (rb[p0 + i] for i in range(4))
            d1, d2, d3 = pltpu.roll(d1, 96, 1), pltpu.roll(d2, 64, 1), pltpu.roll(d3, 32, 1)
            packed = (
                jnp.where(lane8 < 96, d0, d1),
                jnp.where(lane8 < 64, d1, d2),
                jnp.where(lane8 < 32, d2, d3),
            )
            block = []
            q0 = p0 // 4 * 3
            for p, d in enumerate(packed, q0):
                m = mt[:, p * 128 : (p + 1) * 128]
                ends = [x + d * ms[i : i + 1, p * 128 : (p + 1) * 128] for i, x in enumerate(ends)]
                hi = d.astype(BF16).astype(F32)
                rows = [jnp.broadcast_to(v[i : i + 1], (NR, 128)) * m for v in (hi, d - hi) for i in range(8)]
                block.append(jnp.concatenate(rows, axis=0).astype(BF16))
            y = mm_nt(jnp.concatenate(block, axis=1), tt[:, q0 * 128 : (q0 + 3) * 128])
            g = y if g is None else g + y
        g = g[: 8 * NR] + g[8 * NR :]
        hi = g.astype(BF16).astype(F32)
        lo = g - hi
        left = iota((1, 128), 1) < 64
        re, im = [], []
        for j in range(4):
            at = slice(j // 2 * 128, j // 2 * 128 + 128)
            h, l = hi[:, at], pltpu.roll(lo[:, at], 64, 1)
            both = jnp.where(left, h, l) if j % 2 == 0 else jnp.where(left, l, h)
            f = jnp.concatenate([both, h], axis=1).astype(BF16)
            f = mm(f, table("y_even" if j % 2 == 0 else "y_odd"))
            row_re, row_im = [], []
            for z in range(4):
                a = f[(2 * z) * NR : (2 * z + 1) * NR]
                b = f[(2 * z + 1) * NR : (2 * z + 2) * NR]
                row_re.append(a[:, :128] - b[:, 128:])
                row_im.append(a[:, 128:] + b[:, :128])
            re.append(jnp.concatenate(row_re, axis=1))
            im.append(jnp.concatenate(row_im, axis=1))
        rows = re + im
        ex, ey = (jnp.sum(x, axis=1, keepdims=True) for x in ends)
        extra = []
        for z in range(4):
            k = 2 * z
            yr, yi = ey[k : k + 1], ey[k + 1 : k + 2]
            x = jnp.broadcast_to(ex[k : k + 2], (2, 128))
            y = [yr * cos_b - yi * sin_b, yr * sin_b + yi * cos_b]
            extra.append(jnp.concatenate([x] + y + [jnp.zeros((12, 128), F32)], axis=0))
        rows.append(jnp.concatenate(extra, axis=1))
        return mm(table("x_up"), stack_rows(jnp.concatenate(rows, axis=0)))

    dens = None
    for n in range(2):
        arrive(A1 + n)
        f = to_field(rb1.at[n])
        field[n] = f
        term = (f[:128] * f[:128] + f[128:] * f[128:]) * (occ[n] * (1.0 / 16.0))
        dens = term if dens is None else dens + term

    def plane_x(x, name):
        flipped = jnp.concatenate([turned(x[:, z * 128 : (z + 1) * 128]) for z in range(4)], axis=1)
        return mm(table(name), stack_rows(jnp.concatenate([x, flipped], axis=0)))

    def plane_inverse(x, name):
        y = plane_x(x, name)
        return rows_to_lanes(mm(stack_lanes(lanes_to_rows(y)), table("piy")))

    means = []
    for z in range(4):
        means.append(total(dens[:, z * 128 : (z + 1) * 128]) * (1.0 / (NG * NG)))
    mean = jnp.concatenate([jnp.broadcast_to(m, (1, 128)) for m in means], axis=1)
    dens = dens - mean
    xb[...] = plane_x(rows_to_lanes(mm(stack_lanes(lanes_to_rows(dens)), table("py"))), "px")
    head = jnp.where(lax.bitwise_and(iota((8, 512), 1), 127) == 0, mean * float(NG * NG), 0.0)
    xb[0:8] = xb[0:8] + jnp.where(iota((8, 512), 0) == 0, head, 0.0)
    send_band(lambda to: xb.at[pl.ds(pl.multiple_of(16 * to, 16), 16)], rsb.at[band], rsb, RS)

    c0, c1, c2 = (cols[pl.ds(i, 8, stride=3), :] for i in range(3))
    blocks = (
        c0,
        jnp.where(lane8 < 32, pltpu.roll(c0, 32, 1), pltpu.roll(c1, 32, 1)),
        jnp.where(lane8 < 64, pltpu.roll(c1, 64, 1), pltpu.roll(c2, 64, 1)),
        pltpu.roll(c2, 96, 1),
    )
    for i, block in enumerate(blocks):
        cpad[pl.ds(i, 8, stride=4), :] = jnp.where(lane8 < ST, block, -1)
    own = cpad[pl.ds(me, 1), :]
    wx = wrapped(lax.bitwise_and(lax.shift_right_arithmetic(own, 7), 127))
    wy = wrapped(lax.bitwise_and(own, 127))
    reach = wx * wx + wy * wy
    coarse = lax.shift_right_logical(reach, 5).astype(F32)
    fine = lax.bitwise_and(reach, 31).astype(F32)
    both = jnp.concatenate([jnp.broadcast_to(coarse, (8, 128)), jnp.broadcast_to(fine, (8, 128))], axis=0)
    picked = mm(jnp.concatenate([both, both], axis=1).astype(BF16), sh[...])
    wz = wrapped(zval)
    kin[...] = (123.4 / (NG * NG)) * (32.0 * picked[0:1] + picked[8:9] + (wz * wz).astype(F32))

    apad[...] = jnp.full((3, 1024), -1, jnp.int32)
    apad[:, : atoms.shape[1]] = atoms[...]

    def spots(row):
        hot = (iota((128, 1024), 0) == apad[row : row + 1]).astype(BF16)
        return mm(table("circ"), jnp.concatenate([hot, hot], axis=0))

    gz[...] = spots(2)
    gy_hi, gy_lo = split(spots(1))
    gx = spots(0) * FORM
    for z in range(4):
        gl = gx * gz[pl.ds(4 * me + z, 1), :]
        g_hi, g_lo = split(gl)
        vloc[:, z * 128 : (z + 1) * 128] = mm_nt(g_hi, gy_hi) + mm_nt(g_lo, gy_hi) + mm_nt(g_hi, gy_lo)

    lane = iota((128, 256), 1)
    wkz = wrapped(iota((128, 256), 0))
    kx = 16 * band + 2 * lax.div(me, 4) + lax.shift_right_logical(lane, 7)
    lane = lax.bitwise_and(lane, 127)
    wkx = wrapped(kx)
    ky = lax.bitwise_and(lane, 63)
    q = wkz * wkz + wkx * wkx + ky * ky
    corner = jnp.logical_and(q == 0, lane == 64)
    q = jnp.where(corner, 4096, q).astype(F32)
    factor = jnp.where(q > 0.0, (HARTREE / NG**3) / jnp.maximum(q, 1.0), 0.0)

    def transpose(i, carry):
        at = pl.ds(pl.multiple_of(i * 512, 512), 512)
        sht[at, :] = sh[:, at].T
        return carry

    lax.fori_loop(0, NPW_DEV // 512, transpose, 0)
    arrive(RS)
    s = rsb[0]
    for i in range(1, NB):
        s = s + rsb[i]
    sbuf[...] = s
    for i in range(8):
        for z in range(4):
            tb[i, 2 * z : 2 * z + 2, :] = s[2 * i : 2 * i + 2, z * 128 : (z + 1) * 128]
    mine = lax.div(me, 4)
    slot_me = pl.ds(pl.multiple_of(8 * me, 8), 8)
    pltpu.make_async_copy(tb.at[mine], rb2.at[slot_me], rsem.at[A2]).start()

    for offset in PEERS:
        to = peer(offset)
        pltpu.make_async_remote_copy(
            tb.at[lax.div(to, 4)], rb2.at[slot_me], ssem.at[A2], rsem.at[A2], device_id={"pw": to}, device_id_type=MESH
        ).start()
    due[A2], gone[A2] = rb2, rb2.at[pl.ds(0, 8 * (NP - 1))]

    arrive(A2)
    x = [
        jnp.concatenate([rb2[pl.ds(2 * z + k, NP, stride=8), :] for z in range(4)], axis=0) for k in range(2)
    ]
    x = jnp.concatenate(x, axis=1)
    flat = jnp.logical_and(lane == 0, kx == 0)
    x = x - jnp.where(flat, jnp.sum(jnp.where(flat, x, 0.0), axis=0, keepdims=True) * (1.0 / NG), 0.0)
    x = mm(table("pz"), stack_rows(jnp.concatenate([x, turned(x)], axis=0))) * factor
    x = mm(table("piz"), stack_rows(jnp.concatenate([x, turned(x)], axis=0)))
    for z in range(4):
        for k in range(2):
            ub[pl.ds(2 * z + k, NP, stride=8), :] = x[z * NP : (z + 1) * NP, k * 128 : (k + 1) * 128]
    low = lax.rem(me, 4)
    turn = band * 8 + mine
    place = pl.ds(pl.multiple_of(8 * turn, 8), 8)
    pltpu.make_async_copy(ub.at[slot_me], rbv.at[place], rsem.at[A3]).start()

    for away, x, half in TARGETS:
        spot = peer((x, 2 * half, 0))
        pltpu.make_async_remote_copy(
            ub.at[pl.ds(pl.multiple_of(8 * spot, 8), 8)],
            rbv.at[place],
            ssem.at[A3],
            rsem.at[A3],
            device_id={"band": lax.rem(band + away, NB), "pw": spot},
            device_id_type=MESH,
        ).start()
    due[A3], gone[A3] = rbv, rbv.at[pl.ds(0, 8 * 63)]
    arrive(A3)
    vk = [
        jnp.concatenate([rbv[pl.ds(2 * z + k, 64, stride=8), :] for k in range(2)], axis=0) for z in range(4)
    ]
    pot[...] = plane_inverse(jnp.concatenate(vk, axis=1), "pixp") + vloc[...]

    lane1 = iota((8, 128), 1)
    weight = NPW / NG**3
    for n in range(2):
        f = field[n]
        v = pot[...]
        u = jnp.concatenate([v * f[:128], v * f[128:]], axis=0)
        nsq_part = total(coeffs[0, n : n + 1] * coeffs[0, n : n + 1] + coeffs[1, n : n + 1] * coeffs[1, n : n + 1])
        cross_part = weight * total(u[:128] * f[:128] + u[128:] * f[128:]) + total(
            kin[...]
            * (coeffs[0, n : n + 1] * coeffs[0, n : n + 1] + coeffs[1, n : n + 1] * coeffs[1, n : n + 1])
        )
        x = mm(table("x_down"), stack_rows(u))
        tiles = []
        for t in range(2):
            rows = [
                jnp.concatenate(
                    [x[(c * 4 + j) * NR : (c * 4 + j + 1) * NR, z * 128 : (z + 1) * 128] for j in (2 * t, 2 * t + 1)],
                    axis=1,
                )
                for z in range(4)
                for c in range(2)
            ]
            o = mm(stack_lanes(jnp.concatenate(rows, axis=0)), table("y_down"))
            rows = []
            for z in range(4):
                a = o[(2 * z) * NR : (2 * z + 1) * NR]
                b = o[(2 * z + 1) * NR : (2 * z + 2) * NR]
                rows.append(a[:, :128] + b[:, 128:])
                rows.append(b[:, :128] - a[:, 128:])
            tiles.append(jnp.concatenate(rows, axis=0))
        hi, lo = split(jnp.concatenate(tiles, axis=1))
        edge = x[8 * NR :]
        ex, ey = [], []
        for z in range(4):
            a, b, c, d = (edge[i : i + 1, z * 128 : (z + 1) * 128] for i in range(4))
            ex += [a, b]
            ey += [c * cos_b + d * sin_b, d * cos_b - c * sin_b]
        ex, ey = (jnp.sum(jnp.concatenate(v, axis=0), axis=1, keepdims=True) for v in (ex, ey))
        extra = jnp.where(lane1 == 96, nsq_part, 0.0) + jnp.where(lane1 == 97, cross_part, 0.0)

        y = mm(jnp.concatenate([hi, lo], axis=0), tt[...])
        y = y[: 8 * NR] + y[8 * NR :]
        m = mt[...]
        y = jnp.concatenate(
            [jnp.sum(y[k * NR : (k + 1) * NR] * m, axis=0, keepdims=True) for k in range(8)], axis=0
        )
        y = y + ex * ms[0:1] + ey * ms[1:2]
        for g in range(NP // 4):
            t0, t1, t2 = (y[:, (3 * g + i) * 128 : (3 * g + i + 1) * 128] for i in range(3))
            blocks = (
                t0,
                jnp.where(lane8 < 32, pltpu.roll(t0, 32, 1), pltpu.roll(t1, 32, 1)),
                jnp.where(lane8 < 64, pltpu.roll(t1, 64, 1), pltpu.roll(t2, 64, 1)),
                pltpu.roll(t2, 96, 1),
            )
            for i, block in enumerate(blocks):
                sb4[n, 4 * g + i] = jnp.where(lane8 < ST, block, extra)
        send_pw(sb4.at[n], rb4.at[n], A4 + n)

    at_band = pl.ds(pl.multiple_of(16 * band, 16), 16)
    send_band(lambda to: sbuf, dk.at[at_band], dk, AGD)

    states = []
    for n in range(2):
        arrive(A4 + n)
        r = rb4[n]
        ends = jnp.sum(r, axis=0)[0:1]
        nsq = jnp.sum(jnp.where(iota((1, 128), 1) == 96, ends, 0.0), axis=1, keepdims=True) + EPSILON
        cross = jnp.sum(jnp.where(iota((1, 128), 1) == 97, ends, 0.0), axis=1, keepdims=True)
        alpha0 = cross / nsq
        g = mm(table("z_down"), stack_rows(r.reshape(256, 128)))
        hi, lo = split(jnp.concatenate([g[: 2 * KH], g[2 * KH :]], axis=1))
        y = mm(jnp.concatenate([hi, lo], axis=0), sh[...])
        y = y[: 2 * KH] + y[2 * KH :]
        pick = iota((KH, NPW_DEV), 0) == khi
        for c in range(2):
            part = jnp.sum(jnp.where(pick, y[c * KH : (c + 1) * KH], 0.0), axis=0, keepdims=True)
            wvec[n, c : c + 1] = part + (kin[...] - alpha0) * coeffs[c, n : n + 1]
        w_re = wvec[n, 0:1]
        w_im = wvec[n, 1:2]
        sb5[n] = scatter(w_re, w_im, True)
        send_pw(sb5.at[n], rb5.at[n], A5 + n)
        wsq = w_re * w_re + w_im * w_im
        states.append((nsq, alpha0, total(wsq), total(wsq * kin[...])))

    out = jnp.zeros((8, 128), F32)
    for n in range(2):
        arrive(A5 + n)
        f = to_field(rb5.at[n])
        energy = weight * total(pot[...] * (f[:128] * f[:128] + f[128:] * f[128:])) + states[n][3]
        out = out + jnp.where(lane1 == 2 * n, states[n][2], 0.0) + jnp.where(lane1 == 2 * n + 1, energy, 0.0)
    sbr[...] = out[0:1]
    pltpu.make_async_copy(sbr, rbr.at[me], rsem.at[AR]).start()

    for offset in PEERS:
        to = peer(offset)
        pltpu.make_async_remote_copy(
            sbr, rbr.at[me], ssem.at[AR], rsem.at[AR], device_id={"pw": to}, device_id_type=MESH
        ).start()
    due[AR], gone[AR] = rbr, rbr.at[pl.ds(0, NP - 1)]
    arrive(AGD)
    d = plane_inverse(dk[...], "pix") * (1.0 / (NG * NG))
    for z in range(4):
        dens_val[z] = d[:, z * 128 : (z + 1) * 128]
    dens_copy = pltpu.make_async_copy(dens_val, dens_out, osem.at[0])
    dens_copy.start()
    arrive(AR)
    ends = jnp.sum(rbr[...], axis=0)
    for n in range(2):
        nsq, alpha0 = states[n][0], states[n][1]
        ww = jnp.sum(jnp.where(iota((1, 128), 1) == 2 * n, ends, 0.0), axis=1, keepdims=True)
        ew = jnp.sum(jnp.where(iota((1, 128), 1) == 2 * n + 1, ends, 0.0), axis=1, keepdims=True)
        spread_sq = ww / nsq + EPSILON
        spread = jnp.sqrt(spread_sq)
        alpha1 = ew / (nsq * spread_sq)
        first, second = exponential_weights(alpha0, alpha1, spread)
        sec_re = second[0] / spread
        sec_im = second[1] / spread
        c_re, c_im = coeffs[0, n : n + 1], coeffs[1, n : n + 1]
        w_re, w_im = wvec[n, 0:1], wvec[n, 1:2]
        new[0, n : n + 1] = first[0] * c_re - first[1] * c_im + (sec_re * w_re - sec_im * w_im)
        new[1, n : n + 1] = first[0] * c_im + first[1] * c_re + (sec_re * w_im + sec_im * w_re)

    new_copy = pltpu.make_async_copy(new, new_out, osem.at[1])
    new_copy.start()
    finish()
    dens_copy.wait()
    new_copy.wait()


def copies(new_in, dens_in, new_out, dens_out):
    new_out[...] = new_in[...]
    dens_out[...] = dens_in[...]


def local(coeffs, occupation, stick_columns, sphere_slots, atom_sites):
    cols = stick_columns.reshape(NP * ST // 128, 128)
    slots = sphere_slots.reshape(NPW_DEV // 128, 128)
    hbm = pl.BlockSpec(memory_space=pl.ANY)
    vm = pl.BlockSpec(memory_space=pltpu.VMEM)
    tables = [jnp.asarray(TABLES[k]) for k in NAMES]
    V = pltpu.VMEM
    results = (
        jax.ShapeDtypeStruct((2, 2, NPW_DEV), F32),
        jax.ShapeDtypeStruct((4, NG, NG), F32),
    )
    step = pl.pallas_call(
        kernel,
        out_shape=results,
        in_specs=[hbm] * (5 + len(NAMES)),
        out_specs=(hbm, hbm),
        scratch_shapes=[
            V((2, 2, NPW_DEV), F32),
            pltpu.SMEM((2,), F32),
            V((NP * ST // 128, 128), jnp.int32),
            V((NPW_DEV // 128, 128), jnp.int32),
            V(atom_sites.shape, jnp.int32),
            V((2, 2, NPW_DEV), F32),
            V((4, NG, NG), F32),
            V((256, NPW_DEV), BF16),
            V((NPW_DEV, 256), BF16),
            V((4 * KH, NPW_DEV), BF16),
            V((1, NPW_DEV), F32),
            V((256, NQ * 128), BF16),
            V((NR, NQ * 128), F32),
            V((2, NQ * 128), F32),
            V((2, 256, 512), F32),
            V((1, NPW_DEV), jnp.int32),
            V((NP, 128), jnp.int32),
            V((3, 1024), jnp.int32),
            V((128, 512), F32),
            V((128, 512), F32),
            V((2, 2, NPW_DEV), F32),
            V((2, NP, 8, 128), F32),
            V((2, NP, 8, 128), F32),
            V((128, 512), F32),
            V((NB, 16, 512), F32),
            V((16, 512), F32),
            V((8, 8, 128), F32),
            V((8 * NP, 128), F32),
            V((8 * NP, 128), F32),
            V((512, 128), F32),
            V((128, 512), F32),
            V((2, NP, 8, 128), F32),
            V((2, NP, 8, 128), F32),
            V((2, NP, 8, 128), F32),
            V((2, NP, 8, 128), F32),
            V((1, 128), F32),
            V((NP, 1, 128), F32),
            V((128, 1024), F32),
            pltpu.SemaphoreType.DMA((N_SEM,)),
            pltpu.SemaphoreType.DMA((N_SEM,)),
            pltpu.SemaphoreType.DMA((5,)),
            pltpu.SemaphoreType.DMA((2,)),
        ]
        + [V(TABLES[k].shape, BF16) for k in NAMES]
        + [pltpu.SemaphoreType.DMA((len(NAMES),))],
        compiler_params=pltpu.CompilerParams(
            collective_id=0, has_side_effects=True, vmem_limit_bytes=60 * 1024 * 1024
        ),
        name="step",
    )(coeffs, occupation, cols, slots, atom_sites, *tables)
    return pl.pallas_call(
        copies,
        out_shape=results,
        in_specs=[vm, vm],
        out_specs=(vm, vm),
        name="results",
    )(*step)


def solution(mesh):
    in_specs = (P(None, "band", "pw"), P("band"), P(), P("pw"), P())
    out_specs = (P(None, "band", "pw"), P("pw", None, None))
    return jax.shard_map(local, mesh=mesh, in_specs=in_specs, out_specs=out_specs, check_vma=False)
```
